32 devices in a mesh: groups: 2 (over x), et: 16 (over z, y, core).
Axes of the slice: x: 2, y: 2, z: 4, core: 2. Of those that a mesh axis runs over, the one named last changes fastest.
Arguments:
- tokens: bfloat16 [4096, 6144], P(('groups', 'et')), parts along dimension 0, may hold values from -6 to 6
- out_grad: bfloat16 [4096, 6144], P(('groups', 'et')), parts along dimension 0, may hold values from -6 to 6
- expert_ids: int32 [4096, 4], P(('groups', 'et')), parts along dimension 0, may hold values from 0 to 15, as said below
- gate_vals: bfloat16 [4096, 4], P(('groups', 'et')), parts along dimension 0, may hold values from 0.19921875 to 1
- w_gate: bfloat16 [6144, 5376], P(None, 'et'), may hold values from -0.078125 to 0.078125
- w_up: bfloat16 [6144, 5376], P(None, 'et'), may hold values from -0.078125 to 0.078125
- w_down: bfloat16 [5376, 6144], P('et'), may hold values from -0.078125 to 0.078125
Outputs:
- mixed: bfloat16 [4096, 6144], P(('groups', 'et')), parts along dimension 0
- grad_tokens: bfloat16 [4096, 6144], P(('groups', 'et')), parts along dimension 0
- grad_gate: bfloat16 [12288, 5376], P('groups', 'et'), parts along dimension 0
- grad_up: bfloat16 [12288, 5376], P('groups', 'et'), parts along dimension 0
- grad_down: bfloat16 [10752, 6144], P(('groups', 'et')), parts along dimension 0
The draws below stay inside these ranges and needn't reach their ends.
There are 2 independent parts, one for each index of `groups`. The reference program is written for one: setup_inputs(seed, part) draws one part's arguments, and reference() takes and returns one part's arrays. A program takes and returns all parts, laid end to end along the dimension named above; an argument that names none is the same for every part. Nothing has to cross between parts.
Inputs may be any that keep to these rules, and one draw needn't show every extreme that they name: `expert_ids`: each row names 4 different experts of 0 to 15; among the 128 rows of one index of et at most 16 name expert 0, and some index has exactly 16.
All inputs are finite; a program needn't handle non-finite values.
Results may differ from the reference program's by a relative error of at most 0.0051.
Values may be sent and summed in bfloat16 or wider, within the bound.
No kernel may reach another device: no remote copies, remote signals or barrier semaphores. Data moves between devices by JAX's collectives and lax.ppermute only.
A program may use at most 128 MiB of HBM per device.

```python
import jax
import jax.numpy as jnp

D = 6144
FF = 5376
EXPERTS = 16
TOP = 4
TOK_DEV = 128
CAP = 16
TOKENS = 2048


def draw_expert_ids(key, part):
    key = jax.random.fold_in(key, 11)
    key_count, key_top, key_rank, key_other, key_place = jax.random.split(key, 5)
    blocks = TOKENS // TOK_DEV
    counts = jax.random.randint(key_count, (blocks,), max(1, CAP // 3), CAP + 1)
    chosen = jax.random.randint(key_top, (), 0, blocks)
    counts = jnp.where(jnp.arange(blocks) == chosen, CAP, counts)
    scores = jax.random.randint(key_rank, (blocks, TOK_DEV), 0, 1 << 20) * TOK_DEV + jnp.arange(TOK_DEV)[None, :]
    ranking = jnp.argsort(jnp.argsort(scores, axis=1), axis=1)
    routed = (ranking < counts[:, None]).reshape(TOKENS)
    other_scores = jax.random.randint(key_other, (TOKENS, EXPERTS - 1), 0, 1 << 16) * EXPERTS + jnp.arange(EXPERTS - 1)[None, :]
    others = jnp.argsort(other_scores, axis=1)[:, :TOP] + 1
    place = jax.random.randint(key_place, (TOKENS, 1), 0, TOP)
    landed = routed[:, None] & (jnp.arange(TOP)[None, :] == place)
    return jnp.where(landed, 0, others).astype(jnp.int32)


def level_of(rng, shape, shards, smallest, high):
    level = 1.0
    for axis_at, blocks in shards:
        draws = jax.random.uniform(jax.random.fold_in(jax.random.fold_in(rng, 6), axis_at), (blocks,), jnp.float32, smallest / len(shards), high / len(shards))
        level = level * jnp.repeat(jnp.exp(draws), shape[axis_at] // blocks).reshape((-1,) + (1,) * (len(shape) - 1 - axis_at))
    return level


def noise(key, extent, scale, most, cuts=(), dtype=jnp.bfloat16):
    level = level_of(key, extent, cuts, -0.22, 0.18) if cuts else 1.0
    result = jax.random.normal(key, extent, jnp.float32) * scale * level
    return jnp.minimum(jnp.maximum(result, -most), most).astype(dtype)


def setup_inputs(seed: int = 0, part: int = 0) -> dict:
    key_of = jax.random.split(jax.random.key(seed), 8)
    own_keys = jax.random.split(jax.random.fold_in(key_of[7], part), 8)
    tokens = noise(own_keys[0], (TOKENS, D), 1.0, 6.0, ((0, 16),))
    out_grad = noise(own_keys[1], (TOKENS, D), 1.0, 6.0, ((0, 16),))
    expert_ids = draw_expert_ids(jax.random.fold_in(jax.random.fold_in(key_of[7], part), 71), part)
    gate_vals = jnp.clip(0.19921875 + 0.80078125 * jax.random.uniform(own_keys[3], (TOKENS, TOP), jnp.float32) ** level_of(own_keys[3], (TOKENS, TOP), ((0, 16),), -0.2, 0.2), 0.19921875, 1.0).astype(jnp.bfloat16)
    w_gate = noise(key_of[4], (D, FF), D ** -0.5, 0.078125, ((1, 16),))
    w_up = noise(key_of[5], (D, FF), D ** -0.5, 0.078125, ((1, 16),))
    w_down = noise(key_of[6], (FF, D), FF ** -0.5, 0.078125, ((0, 16),))
    return dict(tokens=tokens, out_grad=out_grad, expert_ids=expert_ids, gate_vals=gate_vals, w_gate=w_gate, w_up=w_up, w_down=w_down)


def reference(tokens, out_grad, expert_ids, gate_vals, w_gate, w_up, w_down):
    coef = jnp.sum(jnp.where(expert_ids == 0, gate_vals.astype(jnp.float32), 0.0), axis=1)
    coef = coef.astype(jnp.bfloat16).astype(jnp.float32)[:, None]
    gate = jnp.dot(tokens, w_gate, preferred_element_type=jnp.float32)
    up = jnp.dot(tokens, w_up, preferred_element_type=jnp.float32)
    sig = jax.nn.sigmoid(gate)
    act = gate * sig
    hidden = (coef * act * up).astype(jnp.bfloat16)
    mixed = jnp.dot(hidden, w_down, preferred_element_type=jnp.float32).astype(jnp.bfloat16)
    grad_down = jnp.dot(hidden.T, out_grad, preferred_element_type=jnp.float32).astype(jnp.bfloat16)
    scaled = coef * jnp.dot(out_grad, w_down.T, preferred_element_type=jnp.float32)
    dgate = (scaled * up * sig * (1.0 + gate * (1.0 - sig))).astype(jnp.bfloat16)
    dup = (scaled * act).astype(jnp.bfloat16)
    grad_tokens = (jnp.dot(dgate, w_gate.T, preferred_element_type=jnp.float32)
                   + jnp.dot(dup, w_up.T, preferred_element_type=jnp.float32)).astype(jnp.bfloat16)
    grad_gate = jnp.dot(tokens.T, dgate, preferred_element_type=jnp.float32).astype(jnp.bfloat16)
    grad_up = jnp.dot(tokens.T, dup, preferred_element_type=jnp.float32).astype(jnp.bfloat16)
    return mixed, grad_tokens, grad_gate, grad_up, grad_down
```

```python
import jax
import jax.numpy as jnp
from jax import lax
from jax.sharding import PartitionSpec as P

CAP = 16
LANES = 128


def make_per_device(n):
    ring = n // 4
    core_pairs = [(i, i ^ 1) for i in range(n)]
    y_pairs = [(i, i ^ 2) for i in range(n)]
    up_pairs = [(i, (i + 4) % n) for i in range(n)]
    down_pairs = [((i + 4) % n, i) for i in range(n)]

    def permute(x, pairs):
        return lax.ppermute(x, "et", pairs)

    def gather_rows(block):
        here, there = [], []
        held = block
        for k in range(ring):
            if k:
                held = permute(held, up_pairs)
            other = permute(held, y_pairs)
            pair = jnp.concatenate([held, other], axis=0)
            here.append(pair)
            there.append(permute(pair, core_pairs))
        return jnp.concatenate(here + there, axis=0)

    def scatter_rows(own, sent):
        d = own.shape[1]
        total = own + permute(sent, core_pairs).astype(jnp.float32)
        total = total.reshape(ring, 2, CAP, d)
        carry = None
        for k in range(ring - 1, -1, -1):
            got = permute(total[k, 1].astype(jnp.bfloat16), y_pairs)
            term = total[k, 0] + got.astype(jnp.float32)
            if carry is not None:
                term = term + carry.astype(jnp.float32)
            carry = term.astype(jnp.bfloat16)
            if k:
                carry = permute(carry, down_pairs)
        return carry

    def per_device(tokens, out_grad, expert_ids, gate_vals, w_gate, w_up, w_down):
        d = tokens.shape[1]
        landed = expert_ids == 0
        coef = jnp.sum(jnp.where(landed, gate_vals.astype(jnp.float32), 0.0), axis=1).astype(
            jnp.bfloat16
        )
        routed = jnp.any(landed, axis=1)
        slot = jnp.cumsum(routed.astype(jnp.int32)) - 1
        select = (slot[None, :] == jnp.arange(CAP, dtype=jnp.int32)[:, None]) & routed[None, :]
        select_bf = select.astype(jnp.bfloat16)
        wide = jnp.concatenate(
            [tokens, jnp.broadcast_to(coef[:, None], (coef.shape[0], LANES))], axis=1
        )
        slot_x = jnp.dot(select_bf, wide, preferred_element_type=jnp.float32).astype(jnp.bfloat16)
        slot_dy = jnp.dot(select_bf, out_grad, preferred_element_type=jnp.float32).astype(
            jnp.bfloat16
        )
        rows_wide = gather_rows(slot_x)
        rows_dy = gather_rows(slot_dy)
        rows_x = rows_wide[:, :d]
        coef_rows = rows_wide[:, d : d + 1].astype(jnp.float32)
        half = rows_dy.shape[0] // 2

        gate = jnp.dot(rows_x, w_gate, preferred_element_type=jnp.float32)
        up = jnp.dot(rows_x, w_up, preferred_element_type=jnp.float32)
        sig = jax.nn.sigmoid(gate)
        act = gate * sig
        hidden = (coef_rows * act * up).astype(jnp.bfloat16)
        out_rows = jnp.dot(hidden, w_down, preferred_element_type=jnp.float32)
        out_slots = scatter_rows(out_rows[:half], out_rows[half:].astype(jnp.bfloat16))

        scaled = coef_rows * jnp.dot(rows_dy, w_down.T, preferred_element_type=jnp.float32)
        dgate = (scaled * up * sig * (1.0 + gate * (1.0 - sig))).astype(jnp.bfloat16)
        dup = (scaled * act).astype(jnp.bfloat16)
        dx_rows = jnp.dot(dgate, w_gate.T, preferred_element_type=jnp.float32) + jnp.dot(
            dup, w_up.T, preferred_element_type=jnp.float32
        )
        dx_slots = scatter_rows(dx_rows[:half], dx_rows[half:].astype(jnp.bfloat16))

        grad_down = jnp.dot(hidden.T, rows_dy, preferred_element_type=jnp.float32)
        grad_gate = jnp.dot(rows_x.T, dgate, preferred_element_type=jnp.float32)
        grad_up = jnp.dot(rows_x.T, dup, preferred_element_type=jnp.float32)
        mixed = jnp.dot(select_bf.T, out_slots, preferred_element_type=jnp.float32)
        grad_tokens = jnp.dot(select_bf.T, dx_slots, preferred_element_type=jnp.float32)
        return (
            mixed.astype(jnp.bfloat16),
            grad_tokens.astype(jnp.bfloat16),
            grad_gate.astype(jnp.bfloat16),
            grad_up.astype(jnp.bfloat16),
            grad_down.astype(jnp.bfloat16),
        )

    return per_device


def solution(mesh):
    placed = (
        P(("groups", "et"), None),
        P(("groups", "et"), None),
        P(("groups", "et"), None),
        P(("groups", "et"), None),
        P(None, "et"),
        P(None, "et"),
        P("et", None),
    )
    return jax.shard_map(
        make_per_device(mesh.shape["et"]),
        mesh=mesh,
        in_specs=placed,
        out_specs=(
            P(("groups", "et"), None),
            P(("groups", "et"), None),
            P("groups", "et"),
            P("groups", "et"),
            P(("groups", "et"), None),
        ),
        check_vma=False,
    )
```

```python
import jax
import jax.numpy as jnp
from jax import lax
from jax.sharding import PartitionSpec as P

CAP = 16
LANES = 128


def ring_of(n):
    chips = n // 2
    order = list(range(0, chips, 2)) + list(range(chips - 1, 0, -2))
    right = []
    for at, chip in enumerate(order):
        nxt = order[(at + 1) % chips]
        right += [(2 * chip + core, 2 * nxt + core) for core in (0, 1)]
    return right, [(b, a) for a, b in right]


def make_per_device(n):
    steps = n // 4
    core_pairs = [(i, i ^ 1) for i in range(n)]
    right_pairs, left_pairs = ring_of(n)

    def permute(x, pairs):
        return lax.ppermute(x, "et", pairs)

    def gather_rows(x, dy):
        held_xr = held_xl = x
        held_dr = held_dl = dy
        got_x, got_d = [x], [dy]
        split = 1
        for k in range(1, steps + 1):
            if k == steps - 1:
                split = len(got_x)
                early_x = permute(jnp.concatenate(got_x, axis=0), core_pairs)
                early_d = permute(jnp.concatenate(got_d, axis=0), core_pairs)
            if k == steps:
                held_xr, early_x = lax.optimization_barrier((held_xr, early_x))
                held_dl, early_d = lax.optimization_barrier((held_dl, early_d))
                got_x.append(permute(held_xr, right_pairs))
                got_d.append(permute(held_dl, left_pairs))
            else:
                held_xr = permute(held_xr, right_pairs)
                held_xl = permute(held_xl, left_pairs)
                held_dr = permute(held_dr, right_pairs)
                held_dl = permute(held_dl, left_pairs)
                got_x += [held_xr, held_xl]
                got_d += [held_dr, held_dl]
        late_x = permute(jnp.concatenate(got_x[split:], axis=0), core_pairs)
        late_d = permute(jnp.concatenate(got_d[split:], axis=0), core_pairs)
        return (
            jnp.concatenate(got_x + [early_x, late_x], axis=0),
            jnp.concatenate(got_d + [early_d, late_d], axis=0),
        )

    def pair_sum(own, sent):
        total = own + permute(sent, core_pairs).astype(jnp.float32)
        return total.reshape(2 * steps, CAP, own.shape[1])

    def blocks_at(total, carry, k, far_left):
        blocks = {}
        for way in ("l", "r"):
            if k == steps:
                if (way == "l") != far_left:
                    continue
                block = total[2 * steps - 1]
            else:
                block = total[2 * k - 1 if way == "l" else 2 * k]
            if way in carry:
                block = block + carry[way].astype(jnp.float32)
            blocks[way] = block.astype(jnp.bfloat16)
        return blocks

    def send(blocks):
        return {w: permute(b, left_pairs if w == "l" else right_pairs) for w, b in blocks.items()}

    def final(total, carry):
        done = total[0] + carry["l"].astype(jnp.float32) + carry["r"].astype(jnp.float32)
        return done.astype(jnp.bfloat16)

    def after(value, *marks):
        return lax.optimization_barrier((value,) + marks)[0]

    def per_device(tokens, out_grad, expert_ids, gate_vals, w_gate, w_up, w_down):
        d = tokens.shape[1]
        landed = expert_ids == 0
        coef = jnp.sum(jnp.where(landed, gate_vals.astype(jnp.float32), 0.0), axis=1).astype(
            jnp.bfloat16
        )
        routed = jnp.any(landed, axis=1)
        slot = jnp.cumsum(routed.astype(jnp.int32)) - 1
        select = (slot[None, :] == jnp.arange(CAP, dtype=jnp.int32)[:, None]) & routed[None, :]
        select_bf = select.astype(jnp.bfloat16)
        wide = jnp.concatenate(
            [tokens, jnp.broadcast_to(coef[:, None], (coef.shape[0], LANES))], axis=1
        )
        slot_x = jnp.dot(select_bf, wide, preferred_element_type=jnp.float32).astype(jnp.bfloat16)
        slot_dy = jnp.dot(select_bf, out_grad, preferred_element_type=jnp.float32).astype(
            jnp.bfloat16
        )
        rows_wide, rows_dy = gather_rows(slot_x, slot_dy)
        rows_x = rows_wide[:, :d]
        coef_rows = rows_wide[:, d : d + 1].astype(jnp.float32)
        half = rows_dy.shape[0] // 2

        gate = jnp.dot(rows_x, w_gate, preferred_element_type=jnp.float32)
        up = jnp.dot(rows_x, w_up, preferred_element_type=jnp.float32)
        sig = jax.nn.sigmoid(gate)
        act = gate * sig
        hidden = (coef_rows * act * up).astype(jnp.bfloat16)
        out_rows = jnp.dot(hidden, w_down, preferred_element_type=jnp.float32)
        out_total = pair_sum(out_rows[:half], out_rows[half:].astype(jnp.bfloat16))

        scaled = coef_rows * jnp.dot(rows_dy, w_down.T, preferred_element_type=jnp.float32)
        dgate = (scaled * up * sig * (1.0 + gate * (1.0 - sig))).astype(jnp.bfloat16)
        dup = (scaled * act).astype(jnp.bfloat16)
        dgate, out_total = lax.optimization_barrier((dgate, out_total))
        out_blocks = blocks_at(out_total, {}, steps, True)
        out_carry = send(out_blocks)
        dx_rows = jnp.dot(dgate, w_gate.T, preferred_element_type=jnp.float32) + jnp.dot(
            dup, w_up.T, preferred_element_type=jnp.float32
        )
        dx_total = pair_sum(dx_rows[:half], dx_rows[half:].astype(jnp.bfloat16))
        dx_carry = send(blocks_at(dx_total, {}, steps, False))

        grads = []
        work = [(rows_x, dgate), (rows_x, dup), (hidden, rows_dy)]
        for k in range(steps - 1, 0, -1):
            out_blocks = blocks_at(out_total, out_carry, k, True)
            out_carry = send(out_blocks)
            if work:
                lhs, rhs = work.pop(0)
                marks = list(out_blocks.values())
                if len(grads) == 2:
                    lhs = after(lhs, *marks)
                else:
                    rhs = after(rhs, *marks)
                grads.append(jnp.dot(lhs.T, rhs, preferred_element_type=jnp.float32))
            dx_carry = send(blocks_at(dx_total, dx_carry, k, False))
        for lhs, rhs in work:
            grads.append(jnp.dot(lhs.T, rhs, preferred_element_type=jnp.float32))
        grad_gate, grad_up, grad_down = grads
        out_slots = final(out_total, out_carry)
        dx_slots = final(dx_total, dx_carry)
        mixed = jnp.dot(select_bf.T, out_slots, preferred_element_type=jnp.float32)
        grad_tokens = jnp.dot(select_bf.T, dx_slots, preferred_element_type=jnp.float32)
        return (
            mixed.astype(jnp.bfloat16),
            grad_tokens.astype(jnp.bfloat16),
            grad_gate.astype(jnp.bfloat16),
            grad_up.astype(jnp.bfloat16),
            grad_down.astype(jnp.bfloat16),
        )

    return per_device


def solution(mesh):
    placed = (
        P(("groups", "et"), None),
        P(("groups", "et"), None),
        P(("groups", "et"), None),
        P(("groups", "et"), None),
        P(None, "et"),
        P(None, "et"),
        P("et", None),
    )
    return jax.shard_map(
        make_per_device(mesh.shape["et"]),
        mesh=mesh,
        in_specs=placed,
        out_specs=(
            P(("groups", "et"), None),
            P(("groups", "et"), None),
            P("groups", "et"),
            P("groups", "et"),
            P(("groups", "et"), None),
        ),
        check_vma=False,
    )
```

```python
import jax
import jax.numpy as jnp
from jax import lax
from jax.sharding import PartitionSpec as P

CAP = 16
LANES = 128


def ring_of(n):
    chips = n // 2
    order = list(range(0, chips, 2)) + list(range(chips - 1, 0, -2))
    right = []
    for at, chip in enumerate(order):
        nxt = order[(at + 1) % chips]
        right += [(2 * chip + core, 2 * nxt + core) for core in (0, 1)]
    return right, [(b, a) for a, b in right]


def make_per_device(n):
    steps = n // 4
    core_pairs = [(i, i ^ 1) for i in range(n)]
    right_pairs, left_pairs = ring_of(n)

    def permute(x, pairs):
        return lax.ppermute(x, "et", pairs)

    def gather_rows(x, dy):
        held_xr = held_xl = x
        held_dr = held_dl = dy
        got_x, got_d = [x], [dy]
        for k in range(1, steps):
            held_xr = permute(held_xr, right_pairs)
            held_dl = permute(held_dl, left_pairs)
            held_dr = permute(held_dr, right_pairs)
            held_xl = permute(held_xl, left_pairs)
            got_x += [held_xr, held_xl]
            got_d += [held_dr, held_dl]
        far_x = permute(held_xr, right_pairs)
        far_d = permute(held_dl, left_pairs)
        early_x = permute(jnp.concatenate(got_x, axis=0), core_pairs)
        early_d = permute(jnp.concatenate(got_d, axis=0), core_pairs)
        late_x = permute(far_x, core_pairs)
        late_d = permute(far_d, core_pairs)
        return (
            jnp.concatenate(got_x + [far_x, early_x, late_x], axis=0),
            jnp.concatenate(got_d + [far_d, early_d, late_d], axis=0),
        )

    cut = max(2 * steps - 3, 1) * CAP

    def pair_sum(own, sent):
        far = own[cut:] + permute(sent[cut:], core_pairs).astype(jnp.float32)
        near = own[:cut] + permute(sent[:cut], core_pairs).astype(jnp.float32)
        return near, far

    def block_of(total, at):
        at = at * CAP
        return total[0][at : at + CAP] if at < cut else total[1][at - cut : at - cut + CAP]

    def wave(total, carry, at, far_way):
        blocks = {}
        for way in ("l", "r"):
            k = steps - at + (way == far_way)
            if k < 1:
                continue
            block = block_of(total, 2 * k - (way == "l" or k == steps))
            if way in carry:
                block = block + carry[way].astype(jnp.float32)
            blocks[way] = block.astype(jnp.bfloat16)
        return lax.optimization_barrier(blocks)

    def send(blocks):
        return {w: permute(b, left_pairs if w == "l" else right_pairs) for w, b in blocks.items()}

    def final(total, carry):
        done = block_of(total, 0) + carry["l"].astype(jnp.float32) + carry["r"].astype(jnp.float32)
        return done.astype(jnp.bfloat16)

    def tie(value, blocks):
        ways = list(blocks)
        tied = lax.optimization_barrier((value, *[blocks[w] for w in ways]))
        return tied[0], dict(zip(ways, tied[1:]))

    def per_device(tokens, out_grad, expert_ids, gate_vals, w_gate, w_up, w_down):
        d = tokens.shape[1]
        landed = expert_ids == 0
        coef = jnp.sum(jnp.where(landed, gate_vals.astype(jnp.float32), 0.0), axis=1).astype(
            jnp.bfloat16
        )
        routed = jnp.any(landed, axis=1)
        slot = jnp.cumsum(routed.astype(jnp.int32)) - 1
        select = (slot[None, :] == jnp.arange(CAP, dtype=jnp.int32)[:, None]) & routed[None, :]
        select_bf = select.astype(jnp.bfloat16)
        wide = jnp.concatenate(
            [tokens, jnp.broadcast_to(coef[:, None], (coef.shape[0], LANES))], axis=1
        )
        slot_x = jnp.dot(select_bf, wide, preferred_element_type=jnp.float32).astype(jnp.bfloat16)
        slot_dy = jnp.dot(select_bf, out_grad, preferred_element_type=jnp.float32).astype(
            jnp.bfloat16
        )
        rows_wide, rows_dy = gather_rows(slot_x, slot_dy)
        rows_x = rows_wide[:, :d]
        coef_rows = rows_wide[:, d : d + 1].astype(jnp.float32)
        half = rows_dy.shape[0] // 2

        gate = jnp.dot(rows_x, w_gate, preferred_element_type=jnp.float32)
        up = jnp.dot(rows_x, w_up, preferred_element_type=jnp.float32)
        sig = jax.nn.sigmoid(gate)
        act = gate * sig
        hidden = (coef_rows * act * up).astype(jnp.bfloat16)
        out_rows = jnp.dot(hidden, w_down, preferred_element_type=jnp.float32)
        out_sent = out_rows[half:].astype(jnp.bfloat16)
        rows_dy, out_sent = lax.optimization_barrier((rows_dy, out_sent))
        out_total = pair_sum(out_rows[:half], out_sent)

        dhid = jnp.dot(rows_dy, w_down.T, preferred_element_type=jnp.float32)
        scaled = coef_rows * dhid
        dgate = (scaled * up * sig * (1.0 + gate * (1.0 - sig))).astype(jnp.bfloat16)
        dup = (scaled * act).astype(jnp.bfloat16)
        dgate, blocks = tie(dgate, wave(out_total, {}, 1, "l"))
        out_carry = send(blocks)
        dx_rows = jnp.dot(dgate, w_gate.T, preferred_element_type=jnp.float32) + jnp.dot(
            dup, w_up.T, preferred_element_type=jnp.float32
        )
        dx_sent = dx_rows[half:].astype(jnp.bfloat16)
        dx_sent, out_carry = tie(dx_sent, out_carry)
        dx_total = pair_sum(dx_rows[:half], dx_sent)
        dx_carry = {}

        grads = []
        work = [(rows_x, dgate), (rows_x, dup), (hidden, rows_dy)]
        for at in range(2, steps + 2):
            if at <= steps:
                out_carry.update(send(wave(out_total, out_carry, at, "l")))
            blocks = wave(dx_total, dx_carry, at - 1, "r")
            if at == 2:
                far, out_carry = tie(dx_total[1], out_carry)
                dx_total = (dx_total[0], far)
            if work:
                lhs, rhs = work.pop(0)
                rhs, blocks = tie(rhs, blocks)
                grads.append(jnp.dot(lhs.T, rhs, preferred_element_type=jnp.float32))
            dx_carry.update(send(blocks))
        for lhs, rhs in work:
            grads.append(jnp.dot(lhs.T, rhs, preferred_element_type=jnp.float32))
        grad_gate, grad_up, grad_down = grads
        out_slots = final(out_total, out_carry)
        dx_slots = final(dx_total, dx_carry)
        mixed = jnp.dot(select_bf.T, out_slots, preferred_element_type=jnp.float32)
        grad_tokens = jnp.dot(select_bf.T, dx_slots, preferred_element_type=jnp.float32)
        return (
            mixed.astype(jnp.bfloat16),
            grad_tokens.astype(jnp.bfloat16),
            grad_gate.astype(jnp.bfloat16),
            grad_up.astype(jnp.bfloat16),
            grad_down.astype(jnp.bfloat16),
        )

    return per_device


def solution(mesh):
    placed = (
        P(("groups", "et"), None),
        P(("groups", "et"), None),
        P(("groups", "et"), None),
        P(("groups", "et"), None),
        P(None, "et"),
        P(None, "et"),
        P("et", None),
    )
    return jax.shard_map(
        make_per_device(mesh.shape["et"]),
        mesh=mesh,
        in_specs=placed,
        out_specs=(
            P(("groups", "et"), None),
            P(("groups", "et"), None),
            P("groups", "et"),
            P("groups", "et"),
            P(("groups", "et"), None),
        ),
        check_vma=False,
    )
```

```python
import jax
import jax.numpy as jnp
from jax import lax
from jax.experimental import pallas as pl
from jax.experimental.pallas import tpu as pltpu
from jax.sharding import PartitionSpec as P

CAP = 16
LANES = 128
ANY = pl.BlockSpec(memory_space=pl.ANY)
CONTRACT_ROWS = (((0,), (0,)), ((), ()))
MARK = jax.ShapeDtypeStruct((8, LANES), jnp.float32)


def whole(shape):
    return pl.BlockSpec(shape, lambda j: (0,) * len(shape))


def columns(rows, width):
    return pl.BlockSpec((rows, width), lambda j: (0, j))


def parts_of(d, most):
    width = LANES
    for w in range(LANES, most + 1, LANES):
        if d % w == 0:
            width = w
    return d // width, width


def params(megabytes):
    return pltpu.CompilerParams(vmem_limit_bytes=megabytes << 20)


def select_kernel(x_ref, dy_ref, ids_ref, vals_ref, wide_ref, slot_dy_ref, select_ref):
    j = pl.program_id(0)
    t = x_ref.shape[0]
    width = x_ref.shape[1]

    @pl.when(j == 0)
    def _():
        landed = ids_ref[...] == 0
        coef = jnp.sum(
            jnp.where(landed, vals_ref[...].astype(jnp.float32), 0.0), axis=0, keepdims=True
        )
        coef = coef.astype(jnp.bfloat16).astype(jnp.float32)
        routed = jnp.max(jnp.where(landed, 1.0, 0.0), axis=0, keepdims=True)
        upto = lax.broadcasted_iota(jnp.int32, (t, t), 0) <= lax.broadcasted_iota(
            jnp.int32, (t, t), 1
        )
        seen = jnp.dot(
            jnp.broadcast_to(routed, (CAP, t)).astype(jnp.bfloat16),
            jnp.where(upto, 1.0, 0.0).astype(jnp.bfloat16),
            preferred_element_type=jnp.float32,
        )
        slot = lax.broadcasted_iota(jnp.int32, (CAP, t), 0).astype(jnp.float32) + 1.0
        select = jnp.where((seen == slot) & (routed > 0.0), 1.0, 0.0)
        select_ref[...] = select.astype(jnp.bfloat16)
        slot_coef = jnp.sum(select * coef, axis=1, keepdims=True)
        wide_ref[:, wide_ref.shape[1] - LANES :] = jnp.broadcast_to(
            slot_coef, (CAP, LANES)
        ).astype(jnp.bfloat16)

    select = select_ref[...]
    at = pl.multiple_of(j * width, LANES)
    wide_ref[:, pl.ds(at, width)] = jnp.dot(
        select, x_ref[...], preferred_element_type=jnp.float32
    ).astype(jnp.bfloat16)
    slot_dy_ref[...] = jnp.dot(
        select, dy_ref[...], preferred_element_type=jnp.float32
    ).astype(jnp.bfloat16)


def select_rows(tokens, out_grad, expert_ids, gate_vals):
    t, d = tokens.shape
    top = expert_ids.shape[1]
    parts, width = parts_of(d, 2048)
    return pl.pallas_call(
        select_kernel,
        grid=(parts,),
        in_specs=[columns(t, width), columns(t, width), whole((top, t)), whole((top, t))],
        out_specs=[whole((CAP, d + LANES)), columns(CAP, width), whole((CAP, t))],
        out_shape=[
            jax.ShapeDtypeStruct((CAP, d + LANES), jnp.bfloat16),
            jax.ShapeDtypeStruct((CAP, d), jnp.bfloat16),
            jax.ShapeDtypeStruct((CAP, t), jnp.bfloat16),
        ],
        compiler_params=params(56),
        cost_estimate=pl.CostEstimate(
            flops=4 * CAP * t * d, bytes_accessed=4 * t * d, transcendentals=0
        ),
    )(tokens, out_grad, expert_ids.T, gate_vals.T)


def spread_kernel(marks, own_ref, left_ref, right_ref, select_ref, *refs):
    total = (
        own_ref[...] + left_ref[...].astype(jnp.float32) + right_ref[...].astype(jnp.float32)
    )
    refs[marks][...] = lax.dot_general(
        select_ref[...],
        total.astype(jnp.bfloat16),
        CONTRACT_ROWS,
        preferred_element_type=jnp.float32,
    ).astype(jnp.bfloat16)


def spread_rows(near, carry, select, marks):
    d = near.shape[1]
    t = select.shape[1]
    parts, width = parts_of(d, 2048)
    return pl.pallas_call(
        lambda *refs: spread_kernel(len(marks), *refs),
        grid=(parts,),
        in_specs=[columns(CAP, width)] * 3 + [whole((CAP, t))] + [ANY] * len(marks),
        out_specs=columns(t, width),
        out_shape=jax.ShapeDtypeStruct((t, d), jnp.bfloat16),
        compiler_params=params(16),
        cost_estimate=pl.CostEstimate(
            flops=2 * CAP * t * d, bytes_accessed=2 * t * d, transcendentals=0
        ),
    )(near, carry["l"], carry["r"], select, *marks)


def grads_kernel(sides, marks, rows_ref, *refs):
    outs = refs[sides + marks :]
    rows = rows_ref[...]
    for i in range(sides):
        outs[i][...] = lax.dot_general(
            refs[i][...], rows, CONTRACT_ROWS, preferred_element_type=jnp.float32
        ).astype(jnp.bfloat16)
    outs[sides][...] = jnp.zeros(outs[sides].shape, jnp.float32)


def weight_grads(rows, sides, d, marks):
    r, f = sides[0].shape
    parts, width = parts_of(d, 1024)
    n = len(sides)
    return pl.pallas_call(
        lambda *refs: grads_kernel(n, len(marks), *refs),
        grid=(parts,),
        in_specs=[columns(r, width)] + [whole((r, f))] * n + [ANY] * len(marks),
        out_specs=[columns(f, width)] * n + [whole(MARK.shape)],
        out_shape=[jax.ShapeDtypeStruct((f, d), jnp.bfloat16)] * n + [MARK],
        compiler_params=params(24),
        cost_estimate=pl.CostEstimate(
            flops=2 * n * r * f * d, bytes_accessed=2 * d * (r + n * f), transcendentals=0
        ),
    )(rows, *sides, *marks)


def ring_of(n):
    chips = n // 2
    order = list(range(0, chips, 2)) + list(range(chips - 1, 0, -2))
    right = []
    for at, chip in enumerate(order):
        nxt = order[(at + 1) % chips]
        right += [(2 * chip + core, 2 * nxt + core) for core in (0, 1)]
    return right, [(b, a) for a, b in right]


def make_per_device(n):
    steps = n // 4
    core_pairs = [(i, i ^ 1) for i in range(n)]
    right_pairs, left_pairs = ring_of(n)

    def permute(x, pairs):
        return lax.ppermute(x, "et", pairs)

    def gather_rows(x, dy):
        held_xr = held_xl = x
        held_dr = held_dl = dy
        got_x, got_d = [x], [dy]
        for k in range(1, steps):
            held_xr = permute(held_xr, right_pairs)
            held_dl = permute(held_dl, left_pairs)
            held_dr = permute(held_dr, right_pairs)
            held_xl = permute(held_xl, left_pairs)
            got_x += [held_xr, held_xl]
            got_d += [held_dr, held_dl]
        far_x = permute(held_xr, right_pairs)
        far_d = permute(held_dl, left_pairs)
        early_x = permute(jnp.concatenate(got_x, axis=0), core_pairs)
        early_d = permute(jnp.concatenate(got_d, axis=0), core_pairs)
        late_x = permute(far_x, core_pairs)
        late_d = permute(far_d, core_pairs)
        return (
            jnp.concatenate(got_x + [far_x, early_x, late_x], axis=0),
            jnp.concatenate(got_d + [far_d, early_d, late_d], axis=0),
        )

    cut = max(2 * steps - 3, 1) * CAP

    def pair_sum(own, sent):
        far = own[cut:] + permute(sent[cut:], core_pairs).astype(jnp.float32)
        near = own[:cut] + permute(sent[:cut], core_pairs).astype(jnp.float32)
        return near, far

    def block_of(total, at):
        at = at * CAP
        return total[0][at : at + CAP] if at < cut else total[1][at - cut : at - cut + CAP]

    def wave(total, carry, at, far_way):
        blocks = {}
        for way in ("l", "r"):
            k = steps - at + (way == far_way)
            if k < 1:
                continue
            block = block_of(total, 2 * k - (way == "l" or k == steps))
            if way in carry:
                block = block + carry[way].astype(jnp.float32)
            blocks[way] = block.astype(jnp.bfloat16)
        return lax.optimization_barrier(blocks)

    def send(blocks):
        return {w: permute(b, left_pairs if w == "l" else right_pairs) for w, b in blocks.items()}

    def tie(value, blocks):
        ways = list(blocks)
        tied = lax.optimization_barrier((value, *[blocks[w] for w in ways]))
        return tied[0], dict(zip(ways, tied[1:]))

    def per_device(tokens, out_grad, expert_ids, gate_vals, w_gate, w_up, w_down):
        d = tokens.shape[1]
        slot_x, slot_dy, select = select_rows(tokens, out_grad, expert_ids, gate_vals)
        rows_wide, rows_dy = gather_rows(slot_x, slot_dy)
        rows_x = rows_wide[:, :d]
        coef_rows = rows_wide[:, d : d + 1].astype(jnp.float32)
        half = rows_dy.shape[0] // 2

        gate = jnp.dot(rows_x, w_gate, preferred_element_type=jnp.float32)
        up = jnp.dot(rows_x, w_up, preferred_element_type=jnp.float32)
        sig = jax.nn.sigmoid(gate)
        act = gate * sig
        hidden = (coef_rows * act * up).astype(jnp.bfloat16)
        out_rows = jnp.dot(hidden, w_down, preferred_element_type=jnp.float32)
        out_sent = out_rows[half:].astype(jnp.bfloat16)
        rows_dy, out_sent = lax.optimization_barrier((rows_dy, out_sent))
        out_total = pair_sum(out_rows[:half], out_sent)

        dhid = jnp.dot(rows_dy, w_down.T, preferred_element_type=jnp.float32)
        scaled = coef_rows * dhid
        dgate = (scaled * up * sig * (1.0 + gate * (1.0 - sig))).astype(jnp.bfloat16)
        dup = (scaled * act).astype(jnp.bfloat16)
        dgate, blocks = tie(dgate, wave(out_total, {}, 1, "l"))
        out_carry = send(blocks)
        dx_rows = jnp.dot(dgate, w_gate.T, preferred_element_type=jnp.float32) + jnp.dot(
            dup, w_up.T, preferred_element_type=jnp.float32
        )
        dx_sent = dx_rows[half:].astype(jnp.bfloat16)
        dx_sent, out_carry = tie(dx_sent, out_carry)
        dx_total = pair_sum(dx_rows[:half], dx_sent)
        dx_carry = {}

        for at in range(2, steps + 2):
            out_blocks = {}
            if at <= steps:
                out_blocks = wave(out_total, out_carry, at, "l")
                out_carry.update(send(out_blocks))
            dx_blocks = wave(dx_total, dx_carry, at - 1, "r")
            dx_carry.update(send(dx_blocks))
            if at == 2:
                marks = [*out_blocks.values(), *dx_blocks.values()]
                grad_gate, grad_up, mark = weight_grads(rows_wide, [dgate, dup], d, marks)
                mark, out_carry = tie(mark, out_carry)
            if at == min(3, steps + 1):
                marks = [*out_blocks.values(), *dx_blocks.values(), mark]
                grad_down, mark = weight_grads(rows_dy, [hidden], d, marks)
                if at < steps:
                    mark, out_carry = tie(mark, out_carry)
                else:
                    mark, dx_carry = tie(mark, dx_carry)
        mixed = spread_rows(out_total[0], out_carry, select, [mark])
        grad_tokens = spread_rows(dx_total[0], dx_carry, select, [])
        return (mixed, grad_tokens, grad_gate.T, grad_up.T, grad_down)

    return per_device


def solution(mesh):
    placed = (
        P(("groups", "et"), None),
        P(("groups", "et"), None),
        P(("groups", "et"), None),
        P(("groups", "et"), None),
        P(None, "et"),
        P(None, "et"),
        P("et", None),
    )
    return jax.shard_map(
        make_per_device(mesh.shape["et"]),
        mesh=mesh,
        in_specs=placed,
        out_specs=(
            P(("groups", "et"), None),
            P(("groups", "et"), None),
            P("groups", "et"),
            P("groups", "et"),
            P(("groups", "et"), None),
        ),
        check_vma=False,
    )
```

```python
import jax
import jax.numpy as jnp
from jax import lax
from jax.experimental import pallas as pl
from jax.experimental.pallas import tpu as pltpu
from jax.sharding import PartitionSpec as P

CAP = 16
LANES = 128
ANY = pl.BlockSpec(memory_space=pl.ANY)
MARK = jax.ShapeDtypeStruct((8, LANES), jnp.float32)


def whole(shape):
    return pl.BlockSpec(shape, lambda j: (0,) * len(shape))


def columns(rows, width):
    return pl.BlockSpec((rows, width), lambda j: (0, j))


def parts_of(d, most):
    width = LANES
    for w in range(LANES, most + 1, LANES):
        if d % w == 0:
            width = w
    return d // width, width


def params(megabytes):
    return pltpu.CompilerParams(vmem_limit_bytes=megabytes << 20)


def grad_kernel(marks, side_ref, rows_ref, *refs):
    out_ref, mark_ref = refs[marks:]
    out_ref[...] = jnp.dot(
        side_ref[...], rows_ref[...], preferred_element_type=jnp.float32
    ).astype(jnp.bfloat16)
    mark_ref[...] = jnp.zeros(mark_ref.shape, jnp.float32)


def weight_grad(side, rows, d, marks):
    r, f = side.shape
    parts, width = parts_of(d, 1024)
    return pl.pallas_call(
        lambda *refs: grad_kernel(len(marks), *refs),
        grid=(parts,),
        in_specs=[whole((f, r)), columns(r, width)] + [ANY] * len(marks),
        out_specs=[columns(f, width), whole(MARK.shape)],
        out_shape=[jax.ShapeDtypeStruct((f, d), jnp.bfloat16), MARK],
        compiler_params=params(12),
        cost_estimate=pl.CostEstimate(
            flops=2 * r * f * d, bytes_accessed=2 * d * (r + f), transcendentals=0
        ),
    )(side.T, rows, *marks)


def ring_of(n):
    chips = n // 2
    order = list(range(0, chips, 2)) + list(range(chips - 1, 0, -2))
    right = []
    for at, chip in enumerate(order):
        nxt = order[(at + 1) % chips]
        right += [(2 * chip + core, 2 * nxt + core) for core in (0, 1)]
    return right, [(b, a) for a, b in right]


def make_per_device(n):
    steps = n // 4
    core_pairs = [(i, i ^ 1) for i in range(n)]
    right_pairs, left_pairs = ring_of(n)

    def permute(x, pairs):
        return lax.ppermute(x, "et", pairs)

    def gather_rows(x, dy):
        held_xr, held_xl = permute(x, right_pairs), permute(x, left_pairs)
        held_dr = held_dl = dy
        got_x, got_d = [x, held_xr, held_xl], [dy]
        for k in range(1, steps):
            if k > 1:
                held_xr = permute(held_xr, right_pairs)
                held_xl = permute(held_xl, left_pairs)
                got_x += [held_xr, held_xl]
            held_dl = permute(held_dl, left_pairs)
            held_dr = permute(held_dr, right_pairs)
            got_d += [held_dr, held_dl]
        far_x = permute(held_xr, right_pairs)
        far_d = permute(held_dl, left_pairs)
        early_x = permute(jnp.concatenate(got_x, axis=0), core_pairs)
        early_d = permute(jnp.concatenate(got_d, axis=0), core_pairs)
        late_x = permute(far_x, core_pairs)
        rows_x = jnp.concatenate(got_x + [far_x, early_x, late_x], axis=0)
        return rows_x, got_d, early_d, far_d

    cut = max(2 * steps - 3, 1) * CAP

    def pair_sum(own, sent):
        far = own[cut:] + permute(sent[cut:], core_pairs).astype(jnp.float32)
        near = own[:cut] + permute(sent[:cut], core_pairs).astype(jnp.float32)
        return near, far

    def block_of(total, at):
        at = at * CAP
        return total[0][at : at + CAP] if at < cut else total[1][at - cut : at - cut + CAP]

    def wave(total, carry, at, far_way):
        blocks = {}
        for way in ("l", "r"):
            k = steps - at + (way == far_way)
            if k < 1:
                continue
            block = block_of(total, 2 * k - (way == "l" or k == steps))
            if way in carry:
                block = block + carry[way].astype(jnp.float32)
            blocks[way] = block.astype(jnp.bfloat16)
        return lax.optimization_barrier(blocks)

    def send(blocks):
        return {w: permute(b, left_pairs if w == "l" else right_pairs) for w, b in blocks.items()}

    def final(near, carry):
        done = near[:CAP] + carry["l"].astype(jnp.float32) + carry["r"].astype(jnp.float32)
        return done.astype(jnp.bfloat16)

    def tie(value, blocks):
        ways = list(blocks)
        tied = lax.optimization_barrier((value, *[blocks[w] for w in ways]))
        return tied[0], dict(zip(ways, tied[1:]))

    def per_device(tokens, out_grad, expert_ids, gate_vals, w_gate, w_up, w_down):
        d = tokens.shape[1]
        landed = expert_ids == 0
        coef = jnp.sum(jnp.where(landed, gate_vals.astype(jnp.float32), 0.0), axis=1).astype(
            jnp.bfloat16
        )
        routed = jnp.any(landed, axis=1)
        slot = jnp.cumsum(routed.astype(jnp.int32)) - 1
        select = (slot[None, :] == jnp.arange(CAP, dtype=jnp.int32)[:, None]) & routed[None, :]
        select = select.astype(jnp.bfloat16)
        slot_x, slot_dy, slot_coef = (
            jnp.dot(select, a, preferred_element_type=jnp.float32).astype(jnp.bfloat16)
            for a in (tokens, out_grad, coef[:, None])
        )
        slot_coef = jnp.broadcast_to(slot_coef, (CAP, LANES))
        rows_wide, got_d, early_d, far_d = gather_rows(
            jnp.concatenate([slot_x, slot_coef], axis=1), slot_dy
        )
        rows_x = rows_wide[:, :d]
        coef_rows = rows_wide[:, d : d + 1].astype(jnp.float32)
        half = rows_wide.shape[0] // 2

        gate = jnp.dot(rows_x, w_gate, preferred_element_type=jnp.float32)
        up = jnp.dot(rows_x, w_up, preferred_element_type=jnp.float32)
        sig = jax.nn.sigmoid(gate)
        act = gate * sig
        hidden = (coef_rows * act * up).astype(jnp.bfloat16)
        out_rows = jnp.dot(hidden, w_down, preferred_element_type=jnp.float32)
        out_sent = out_rows[half:].astype(jnp.bfloat16)
        out_rows, far_d = lax.optimization_barrier((out_rows, far_d))
        out_total = pair_sum(out_rows[:half], out_sent)
        rows_dy = jnp.concatenate(got_d + [far_d, early_d, permute(far_d, core_pairs)], axis=0)

        dhid = jnp.dot(rows_dy, w_down.T, preferred_element_type=jnp.float32)
        scaled = coef_rows * dhid
        dgate = (scaled * up * sig * (1.0 + gate * (1.0 - sig))).astype(jnp.bfloat16)
        dup = (scaled * act).astype(jnp.bfloat16)
        dgate, blocks = tie(dgate, wave(out_total, {}, 1, "l"))
        out_carry = send(blocks)
        dx_rows = jnp.dot(dgate, w_gate.T, preferred_element_type=jnp.float32) + jnp.dot(
            dup, w_up.T, preferred_element_type=jnp.float32
        )
        dx_sent = dx_rows[half:].astype(jnp.bfloat16)
        dx_sent, out_carry = tie(dx_sent, out_carry)
        dx_total = pair_sum(dx_rows[:half], dx_sent)
        dx_carry = {}

        grads, marks = [], []
        work = [(dgate, rows_wide), (dup, rows_wide), (hidden, rows_dy)]
        for at in range(2, steps + 2):
            if at <= steps:
                out_carry.update(send(wave(out_total, out_carry, at, "l")))
            dx_blocks = wave(dx_total, dx_carry, at - 1, "r")
            if work:
                side, rows = work.pop(0)
                side, dx_blocks = tie(side, dx_blocks)
                grad, mark = weight_grad(side, rows, d, marks)
                grads.append(grad)
                if work and at <= steps:
                    mark, out_carry = tie(mark, out_carry)
                marks = [mark]
            dx_carry.update(send(dx_blocks))
        for side, rows in work:
            grads.append(weight_grad(side, rows, d, marks)[0])
        grad_gate, grad_up, grad_down = grads
        mixed, grad_tokens = (
            jnp.dot(select.T, final(total[0], carry), preferred_element_type=jnp.float32).astype(
                jnp.bfloat16
            )
            for total, carry in ((out_total, out_carry), (dx_total, dx_carry))
        )
        return (mixed, grad_tokens, grad_gate.T, grad_up.T, grad_down)

    return per_device


def solution(mesh):
    placed = (
        P(("groups", "et"), None),
        P(("groups", "et"), None),
        P(("groups", "et"), None),
        P(("groups", "et"), None),
        P(None, "et"),
        P(None, "et"),
        P("et", None),
    )
    return jax.shard_map(
        make_per_device(mesh.shape["et"]),
        mesh=mesh,
        in_specs=placed,
        out_specs=(
            P(("groups", "et"), None),
            P(("groups", "et"), None),
            P("groups", "et"),
            P("groups", "et"),
            P(("groups", "et"), None),
        ),
        check_vma=False,
    )
```

```python
import jax
import jax.numpy as jnp
from jax import lax
from jax.experimental import pallas as pl
from jax.experimental.pallas import tpu as pltpu
from jax.sharding import PartitionSpec as P

CAP = 16
LANES = 128
ANY = pl.BlockSpec(memory_space=pl.ANY)
MARK = jax.ShapeDtypeStruct((8, LANES), jnp.float32)


def parts_of(d, most):
    width = LANES
    for w in range(LANES, most + 1, LANES):
        if d % w == 0:
            width = w
    return d // width, width


def params(megabytes):
    return pltpu.CompilerParams(vmem_limit_bytes=megabytes << 20)


def grad_kernel(parts, width, marks, side_ref, rows_ref, *refs):
    out_ref, mark_ref, rows_buf, out_buf, load_sem, store_sem = refs[marks:]
    spans = [pl.ds(j * width, width) for j in range(parts)]
    loads = [
        pltpu.make_async_copy(rows_ref.at[:, at], rows_buf.at[:, at], load_sem.at[j])
        for j, at in enumerate(spans)
    ]
    stores = [
        pltpu.make_async_copy(out_buf.at[:, at], out_ref.at[:, at], store_sem.at[j])
        for j, at in enumerate(spans)
    ]
    for load in loads:
        load.start()
    mark_ref[...] = jnp.zeros(mark_ref.shape, jnp.float32)
    side = side_ref[...]
    for j, at in enumerate(spans):
        loads[j].wait()
        out_buf[:, at] = jnp.dot(
            side, rows_buf[:, at], preferred_element_type=jnp.float32
        ).astype(jnp.bfloat16)
        stores[j].start()
    for store in stores:
        store.wait()


def weight_grad(side, rows, d, marks):
    r, f = side.shape
    parts, width = parts_of(d, 1024)
    return pl.pallas_call(
        lambda *refs: grad_kernel(parts, width, len(marks), *refs),
        in_specs=[pl.BlockSpec(memory_space=pltpu.VMEM), ANY] + [ANY] * len(marks),
        out_specs=[ANY, pl.BlockSpec(memory_space=pltpu.VMEM)],
        out_shape=[jax.ShapeDtypeStruct((f, d), jnp.bfloat16), MARK],
        scratch_shapes=[
            pltpu.VMEM((r, d), jnp.bfloat16),
            pltpu.VMEM((f, d), jnp.bfloat16),
            pltpu.SemaphoreType.DMA((parts,)),
            pltpu.SemaphoreType.DMA((parts,)),
        ],
        compiler_params=params(20),
        cost_estimate=pl.CostEstimate(
            flops=2 * r * f * d, bytes_accessed=2 * d * (r + f), transcendentals=0
        ),
    )(side.T, rows, *marks)


def ring_of(n):
    chips = n // 2
    order = list(range(0, chips, 2)) + list(range(chips - 1, 0, -2))
    right = []
    for at, chip in enumerate(order):
        nxt = order[(at + 1) % chips]
        right += [(2 * chip + core, 2 * nxt + core) for core in (0, 1)]
    return right, [(b, a) for a, b in right]


def make_per_device(n):
    steps = n // 4
    core_pairs = [(i, i ^ 1) for i in range(n)]
    right_pairs, left_pairs = ring_of(n)

    def permute(x, pairs):
        return lax.ppermute(x, "et", pairs)

    def far_block(held_r, held_l):
        at = held_r.shape[1] // 2 // LANES * LANES
        return jnp.concatenate(
            [permute(held_r[:, :at], right_pairs), permute(held_l[:, at:], left_pairs)], axis=1
        )

    def gather_rows(x, dy):
        held_xr = held_xl = x
        held_dr = held_dl = dy
        got_x, got_d = [x], [dy]
        for k in range(1, steps):
            held_xr = permute(held_xr, right_pairs)
            held_xl = permute(held_xl, left_pairs)
            held_dr = permute(held_dr, right_pairs)
            held_dl = permute(held_dl, left_pairs)
            got_x += [held_xr, held_xl]
            got_d += [held_dr, held_dl]
        got_d.append(far_block(held_dr, held_dl))
        far_x = far_block(held_xr, held_xl)
        early_x = permute(jnp.concatenate(got_x, axis=0), core_pairs)
        late_x = permute(far_x, core_pairs)
        rows_x = jnp.concatenate(got_x + [far_x, early_x, late_x], axis=0)
        chip_d = jnp.concatenate(got_d, axis=0)
        return rows_x, jnp.concatenate([chip_d, permute(chip_d, core_pairs)], axis=0)

    cut = max(2 * steps - 3, 1) * CAP

    def pair_sum(own, sent):
        far = own[cut:] + permute(sent[cut:], core_pairs).astype(jnp.float32)
        near = own[:cut] + permute(sent[:cut], core_pairs).astype(jnp.float32)
        return near, far

    def block_of(total, at):
        at = at * CAP
        return total[0][at : at + CAP] if at < cut else total[1][at - cut : at - cut + CAP]

    def wave(total, carry, at, far_way):
        blocks = {}
        for way in ("l", "r"):
            k = steps - at + (way == far_way)
            if k < 1:
                continue
            block = block_of(total, 2 * k - (way == "l" or k == steps))
            if way in carry:
                block = block + carry[way].astype(jnp.float32)
            blocks[way] = block.astype(jnp.bfloat16)
        return lax.optimization_barrier(blocks)

    def send(blocks):
        return {w: permute(b, left_pairs if w == "l" else right_pairs) for w, b in blocks.items()}

    def final(near, carry):
        done = near[:CAP] + carry["l"].astype(jnp.float32) + carry["r"].astype(jnp.float32)
        return done.astype(jnp.bfloat16)

    def tie(value, blocks):
        ways = list(blocks)
        tied = lax.optimization_barrier((value, *[blocks[w] for w in ways]))
        return tied[0], dict(zip(ways, tied[1:]))

    def per_device(tokens, out_grad, expert_ids, gate_vals, w_gate, w_up, w_down):
        d = tokens.shape[1]
        landed = expert_ids == 0
        coef = jnp.sum(jnp.where(landed, gate_vals.astype(jnp.float32), 0.0), axis=1).astype(
            jnp.bfloat16
        )
        routed = jnp.any(landed, axis=1)
        slot = jnp.cumsum(routed.astype(jnp.int32)) - 1
        select = (slot[None, :] == jnp.arange(CAP, dtype=jnp.int32)[:, None]) & routed[None, :]
        select = select.astype(jnp.bfloat16)
        slot_x, slot_dy, slot_coef = (
            jnp.dot(select, a, preferred_element_type=jnp.float32).astype(jnp.bfloat16)
            for a in (tokens, out_grad, coef[:, None])
        )
        slot_coef = jnp.broadcast_to(slot_coef, (CAP, LANES))
        rows_wide, rows_dy = gather_rows(
            jnp.concatenate([slot_x, slot_coef], axis=1), slot_dy
        )
        rows_x = rows_wide[:, :d]
        coef_rows = rows_wide[:, d : d + 1].astype(jnp.float32)
        half = rows_wide.shape[0] // 2

        gate = jnp.dot(rows_x, w_gate, preferred_element_type=jnp.float32)
        up = jnp.dot(rows_x, w_up, preferred_element_type=jnp.float32)
        sig = jax.nn.sigmoid(gate)
        act = gate * sig
        hidden = (coef_rows * act * up).astype(jnp.bfloat16)
        out_rows = jnp.dot(hidden, w_down, preferred_element_type=jnp.float32)
        out_sent = out_rows[half:].astype(jnp.bfloat16)
        rows_dy, out_sent = lax.optimization_barrier((rows_dy, out_sent))
        out_total = pair_sum(out_rows[:half], out_sent)

        dhid = jnp.dot(rows_dy, w_down.T, preferred_element_type=jnp.float32)
        scaled = coef_rows * dhid
        dgate = (scaled * up * sig * (1.0 + gate * (1.0 - sig))).astype(jnp.bfloat16)
        dup = (scaled * act).astype(jnp.bfloat16)
        dgate, blocks = tie(dgate, wave(out_total, {}, 1, "l"))
        out_carry = send(blocks)
        dx_rows = jnp.dot(dgate, w_gate.T, preferred_element_type=jnp.float32) + jnp.dot(
            dup, w_up.T, preferred_element_type=jnp.float32
        )
        dx_sent = dx_rows[half:].astype(jnp.bfloat16)
        dx_sent, out_carry = tie(dx_sent, out_carry)
        dx_total = pair_sum(dx_rows[:half], dx_sent)
        dx_carry = {}

        grads, marks = [], []
        work = [(dgate, rows_wide), (dup, rows_wide), (hidden, rows_dy)]
        for at in range(2, steps + 2):
            if at <= steps:
                out_carry.update(send(wave(out_total, out_carry, at, "l")))
            dx_blocks = wave(dx_total, dx_carry, at - 1, "r")
            if work and at in (2, 3, steps + 1):
                side, rows = work.pop(0)
                side, dx_blocks = tie(side, dx_blocks)
                grad, mark = weight_grad(side, rows, d, marks)
                grads.append(grad)
                if work and at <= steps:
                    mark, out_carry = tie(mark, out_carry)
                marks = [mark]
            dx_carry.update(send(dx_blocks))
        for side, rows in work:
            grads.append(weight_grad(side, rows, d, marks)[0])
        grad_gate, grad_up, grad_down = grads
        mixed, grad_tokens = (
            jnp.dot(select.T, final(total[0], carry), preferred_element_type=jnp.float32).astype(
                jnp.bfloat16
            )
            for total, carry in ((out_total, out_carry), (dx_total, dx_carry))
        )
        return (mixed, grad_tokens, grad_gate.T, grad_up.T, grad_down)

    return per_device


def solution(mesh):
    placed = (
        P(("groups", "et"), None),
        P(("groups", "et"), None),
        P(("groups", "et"), None),
        P(("groups", "et"), None),
        P(None, "et"),
        P(None, "et"),
        P("et", None),
    )
    return jax.shard_map(
        make_per_device(mesh.shape["et"]),
        mesh=mesh,
        in_specs=placed,
        out_specs=(
            P(("groups", "et"), None),
            P(("groups", "et"), None),
            P("groups", "et"),
            P("groups", "et"),
            P(("groups", "et"), None),
        ),
        check_vma=False,
    )
```

```python
import jax
import jax.numpy as jnp
from jax import lax
from jax.experimental import pallas as pl
from jax.experimental.pallas import tpu as pltpu
from jax.sharding import PartitionSpec as P

CAP = 16
LANES = 128
ANY = pl.BlockSpec(memory_space=pl.ANY)
MARK = jax.ShapeDtypeStruct((8, LANES), jnp.float32)


def parts_of(d, most):
    width = LANES
    for w in range(LANES, most + 1, LANES):
        if d % w == 0:
            width = w
    return d // width, width


def params(megabytes):
    return pltpu.CompilerParams(vmem_limit_bytes=megabytes << 20)


def grad_kernel(parts, width, marks, side_ref, rows_ref, *refs):
    out_ref, mark_ref, rows_buf, out_buf, load_sem, store_sem = refs[marks:]
    spans = [pl.ds(j * width, width) for j in range(parts)]
    loads = [
        pltpu.make_async_copy(rows_ref.at[:, at], rows_buf.at[:, at], load_sem.at[j])
        for j, at in enumerate(spans)
    ]
    stores = [
        pltpu.make_async_copy(out_buf.at[:, at], out_ref.at[:, at], store_sem.at[j])
        for j, at in enumerate(spans)
    ]
    for load in loads:
        load.start()
    mark_ref[...] = jnp.zeros(mark_ref.shape, jnp.float32)
    side = side_ref[...]
    for j, at in enumerate(spans):
        loads[j].wait()
        out_buf[:, at] = jnp.dot(
            side, rows_buf[:, at], preferred_element_type=jnp.float32
        ).astype(jnp.bfloat16)
        stores[j].start()
    for store in stores:
        store.wait()


def weight_grad(side, rows, d, marks):
    r, f = side.shape
    parts, width = parts_of(d, 1024)
    return pl.pallas_call(
        lambda *refs: grad_kernel(parts, width, len(marks), *refs),
        in_specs=[pl.BlockSpec(memory_space=pltpu.VMEM), ANY] + [ANY] * len(marks),
        out_specs=[ANY, pl.BlockSpec(memory_space=pltpu.VMEM)],
        out_shape=[jax.ShapeDtypeStruct((f, d), jnp.bfloat16), MARK],
        scratch_shapes=[
            pltpu.VMEM((r, d), jnp.bfloat16),
            pltpu.VMEM((f, d), jnp.bfloat16),
            pltpu.SemaphoreType.DMA((parts,)),
            pltpu.SemaphoreType.DMA((parts,)),
        ],
        compiler_params=params(20),
        cost_estimate=pl.CostEstimate(
            flops=2 * r * f * d, bytes_accessed=2 * d * (r + f), transcendentals=0
        ),
    )(side.T, rows, *marks)


def ring_of(n):
    chips = n // 2
    order = list(range(0, chips, 2)) + list(range(chips - 1, 0, -2))
    right = []
    for at, chip in enumerate(order):
        nxt = order[(at + 1) % chips]
        right += [(2 * chip + core, 2 * nxt + core) for core in (0, 1)]
    return right, [(b, a) for a, b in right]


def make_per_device(n):
    steps = n // 4
    core_pairs = [(i, i ^ 1) for i in range(n)]
    right_pairs, left_pairs = ring_of(n)

    def permute(x, pairs):
        return lax.ppermute(x, "et", pairs)

    def far_block(held_r, held_l):
        at = held_r.shape[1] // 2 // LANES * LANES
        return jnp.concatenate(
            [permute(held_r[:, :at], right_pairs), permute(held_l[:, at:], left_pairs)], axis=1
        )

    def gather_rows(x, dy):
        held_xr = held_xl = x
        held_dr = held_dl = dy
        got_x, got_d = [x], [dy]
        for k in range(1, steps):
            held_xr = permute(held_xr, right_pairs)
            held_xl = permute(held_xl, left_pairs)
            held_dr = permute(held_dr, right_pairs)
            held_dl = permute(held_dl, left_pairs)
            got_x += [held_xr, held_xl]
            got_d += [held_dr, held_dl]
        got_d.append(far_block(held_dr, held_dl))
        far_x = far_block(held_xr, held_xl)
        early_x = permute(jnp.concatenate(got_x, axis=0), core_pairs)
        late_x = permute(far_x, core_pairs)
        chip_d = jnp.concatenate(got_d, axis=0)
        chip_d, late_x = lax.optimization_barrier((chip_d, late_x))
        rows_x = jnp.concatenate(got_x + [far_x, early_x, late_x], axis=0)
        return rows_x, jnp.concatenate([chip_d, permute(chip_d, core_pairs)], axis=0)

    half = 2 * steps * CAP
    cut = max(2 * steps - 3, 1) * CAP

    def far_sum(own, sent):
        return own[cut:half] + permute(sent[cut:], core_pairs).astype(jnp.float32)

    def near_sums(owns, sents):
        near = permute(jnp.concatenate([sent[:cut] for sent in sents], axis=0), core_pairs)
        return [
            own[:cut] + near[i * cut : (i + 1) * cut].astype(jnp.float32)
            for i, own in enumerate(owns)
        ]

    def block_of(total, at):
        at = at * CAP
        return total[0][at : at + CAP] if at < cut else total[1][at - cut : at - cut + CAP]

    def wave(total, carry, at, far_way):
        blocks = {}
        for way in ("l", "r"):
            k = steps - at + (way == far_way)
            if k < 1:
                continue
            block = block_of(total, 2 * k - (way == "l" or k == steps))
            if way in carry:
                block = block + carry[way].astype(jnp.float32)
            blocks[way] = block.astype(jnp.bfloat16)
        return lax.optimization_barrier(blocks)

    def send(blocks):
        return {w: permute(b, left_pairs if w == "l" else right_pairs) for w, b in blocks.items()}

    def final(near, carry):
        done = near[:CAP] + carry["l"].astype(jnp.float32) + carry["r"].astype(jnp.float32)
        return done.astype(jnp.bfloat16)

    def tie(value, blocks):
        ways = list(blocks)
        tied = lax.optimization_barrier((value, *[blocks[w] for w in ways]))
        return tied[0], dict(zip(ways, tied[1:]))

    def per_device(tokens, out_grad, expert_ids, gate_vals, w_gate, w_up, w_down):
        d = tokens.shape[1]
        landed = expert_ids == 0
        coef = jnp.sum(jnp.where(landed, gate_vals.astype(jnp.float32), 0.0), axis=1).astype(
            jnp.bfloat16
        )
        routed = jnp.any(landed, axis=1)
        slot = jnp.cumsum(routed.astype(jnp.int32)) - 1
        select = (slot[None, :] == jnp.arange(CAP, dtype=jnp.int32)[:, None]) & routed[None, :]
        select = select.astype(jnp.bfloat16)
        slot_x, slot_dy, slot_coef = (
            jnp.dot(select, a, preferred_element_type=jnp.float32).astype(jnp.bfloat16)
            for a in (tokens, out_grad, coef[:, None])
        )
        slot_coef = jnp.broadcast_to(slot_coef, (CAP, LANES))
        rows_wide, rows_dy = gather_rows(
            jnp.concatenate([slot_x, slot_coef], axis=1), slot_dy
        )
        rows_x = rows_wide[:, :d]
        coef_rows = rows_wide[:, d : d + 1].astype(jnp.float32)

        gate = jnp.dot(rows_x, w_gate, preferred_element_type=jnp.float32)
        up = jnp.dot(rows_x, w_up, preferred_element_type=jnp.float32)
        sig = jax.nn.sigmoid(gate)
        act = gate * sig
        hidden = (coef_rows * act * up).astype(jnp.bfloat16)
        dhid = jnp.dot(rows_dy, w_down.T, preferred_element_type=jnp.float32)
        scaled = coef_rows * dhid
        dgate = (scaled * up * sig * (1.0 + gate * (1.0 - sig))).astype(jnp.bfloat16)
        dup = (scaled * act).astype(jnp.bfloat16)
        dx_rows = jnp.dot(dgate, w_gate.T, preferred_element_type=jnp.float32) + jnp.dot(
            dup, w_up.T, preferred_element_type=jnp.float32
        )
        dx_sent = dx_rows[half:].astype(jnp.bfloat16)
        hidden, dx_sent = lax.optimization_barrier((hidden, dx_sent))
        dx_far = far_sum(dx_rows, dx_sent)
        out_rows = jnp.dot(hidden, w_down, preferred_element_type=jnp.float32)
        out_sent = out_rows[half:].astype(jnp.bfloat16)
        out_far = far_sum(out_rows, out_sent)
        dx_near, out_near = near_sums([dx_rows, out_rows], [dx_sent, out_sent])
        dx_total, out_total = (dx_near, dx_far), (out_near, out_far)

        dx_carry, out_carry = {}, {}
        grads, marks = [], []
        work = [(dgate, rows_wide), (dup, rows_wide), (hidden, rows_dy)]
        for at in range(1, steps + 1):
            dx_blocks = wave(dx_total, dx_carry, at, "r")
            out_blocks = wave(out_total, out_carry, at, "l")
            if work:
                side, rows = work.pop(0)
                side, dx_blocks = tie(side, dx_blocks)
                grad, mark = weight_grad(side, rows, d, marks)
                grads.append(grad)
                if work and at < steps:
                    mark, dx_carry = tie(mark, dx_carry)
                marks = [mark]
            dx_carry.update(send(dx_blocks))
            out_carry.update(send(out_blocks))
        for side, rows in work:
            grads.append(weight_grad(side, rows, d, marks)[0])
        grad_gate, grad_up, grad_down = grads
        mixed, grad_tokens = (
            jnp.dot(select.T, final(total[0], carry), preferred_element_type=jnp.float32).astype(
                jnp.bfloat16
            )
            for total, carry in ((out_total, out_carry), (dx_total, dx_carry))
        )
        return (mixed, grad_tokens, grad_gate.T, grad_up.T, grad_down)

    return per_device


def solution(mesh):
    placed = (
        P(("groups", "et"), None),
        P(("groups", "et"), None),
        P(("groups", "et"), None),
        P(("groups", "et"), None),
        P(None, "et"),
        P(None, "et"),
        P("et", None),
    )
    return jax.shard_map(
        make_per_device(mesh.shape["et"]),
        mesh=mesh,
        in_specs=placed,
        out_specs=(
            P(("groups", "et"), None),
            P(("groups", "et"), None),
            P("groups", "et"),
            P("groups", "et"),
            P(("groups", "et"), None),
        ),
        check_vma=False,
    )
```

```python
import jax
import jax.numpy as jnp
from jax import lax
from jax.experimental import pallas as pl
from jax.experimental.pallas import tpu as pltpu
from jax.sharding import PartitionSpec as P

CAP = 16
LANES = 128
ANY = pl.BlockSpec(memory_space=pl.ANY)
MARK = jax.ShapeDtypeStruct((8, LANES), jnp.float32)


def parts_of(d, most):
    width = LANES
    for w in range(LANES, most + 1, LANES):
        if d % w == 0:
            width = w
    return d // width, width


def params(megabytes):
    return pltpu.CompilerParams(vmem_limit_bytes=megabytes << 20)


def grad_kernel(parts, width, offset, marks, side_ref, rows_ref, *refs):
    out_ref, mark_ref, rows_buf, out_buf, load_sem, store_sem = refs[marks:]
    spans = [pl.ds(j * width, width) for j in range(parts)]
    loads = [
        pltpu.make_async_copy(
            rows_ref.at[:, pl.ds(offset + j * width, width)], rows_buf.at[:, at], load_sem.at[j]
        )
        for j, at in enumerate(spans)
    ]
    stores = [
        pltpu.make_async_copy(out_buf.at[:, at], out_ref.at[:, at], store_sem.at[j])
        for j, at in enumerate(spans)
    ]
    for load in loads:
        load.start()
    mark_ref[...] = jnp.zeros(mark_ref.shape, jnp.float32)
    side = side_ref[...]
    for j, at in enumerate(spans):
        loads[j].wait()
        out_buf[:, at] = jnp.dot(
            side, rows_buf[:, at], preferred_element_type=jnp.float32
        ).astype(jnp.bfloat16)
        stores[j].start()
    for store in stores:
        store.wait()


def weight_grad(side, rows, offset, d, marks):
    r, f = side.shape
    parts, width = parts_of(d, 1024)
    return pl.pallas_call(
        lambda *refs: grad_kernel(parts, width, offset, len(marks), *refs),
        in_specs=[pl.BlockSpec(memory_space=pltpu.VMEM), ANY] + [ANY] * len(marks),
        out_specs=[ANY, pl.BlockSpec(memory_space=pltpu.VMEM)],
        out_shape=[jax.ShapeDtypeStruct((f, d), jnp.bfloat16), MARK],
        scratch_shapes=[
            pltpu.VMEM((r, d), jnp.bfloat16),
            pltpu.VMEM((f, d), jnp.bfloat16),
            pltpu.SemaphoreType.DMA((parts,)),
            pltpu.SemaphoreType.DMA((parts,)),
        ],
        compiler_params=params(20),
        cost_estimate=pl.CostEstimate(
            flops=2 * r * f * d, bytes_accessed=2 * d * (r + f), transcendentals=0
        ),
    )(side.T, rows, *marks)


def ring_of(n):
    chips = n // 2
    order = list(range(0, chips, 2)) + list(range(chips - 1, 0, -2))
    right = []
    for at, chip in enumerate(order):
        nxt = order[(at + 1) % chips]
        right += [(2 * chip + core, 2 * nxt + core) for core in (0, 1)]
    return right, [(b, a) for a, b in right]


def make_per_device(n):
    steps = n // 4
    core_pairs = [(i, i ^ 1) for i in range(n)]
    right_pairs, left_pairs = ring_of(n)
    blocks = 2 * steps
    near = max(blocks - 3, 1)

    def permute(x, pairs):
        return lax.ppermute(x, "et", pairs)

    def both_ways(right, left):
        return permute(right, right_pairs), permute(left, left_pairs)

    def gather(first, held, wide):
        got = [first, *held]
        for _ in range(2, steps):
            held = both_ways(*held)
            got += held
        far = both_ways(held[0][:, :wide], held[1][:, wide:])
        return got, far

    def early_of(got):
        return permute(jnp.concatenate(got, axis=0), core_pairs)

    def all_rows(got, far, early):
        far = jnp.concatenate(far, axis=1)
        return jnp.concatenate([*got, far, early, permute(far, core_pairs)], axis=0)

    def products(rows, wide, w_gate, w_up, w_down):
        rows_x, rows_dy = rows[:, : wide - LANES], rows[:, wide:]
        coef = rows[:, wide - LANES : wide - LANES + 1].astype(jnp.float32)
        gate = jnp.dot(rows_x, w_gate, preferred_element_type=jnp.float32)
        up = jnp.dot(rows_x, w_up, preferred_element_type=jnp.float32)
        sig = jax.nn.sigmoid(gate)
        act = gate * sig
        hidden = (coef * act * up).astype(jnp.bfloat16)
        scaled = coef * jnp.dot(rows_dy, w_down.T, preferred_element_type=jnp.float32)
        dgate = (scaled * up * sig * (1.0 + gate * (1.0 - sig))).astype(jnp.bfloat16)
        dup = (scaled * act).astype(jnp.bfloat16)
        return hidden, dgate, dup

    def rows_of(hidden, dgate, dup, w_gate, w_up, w_down):
        out_rows = jnp.dot(hidden, w_down, preferred_element_type=jnp.float32)
        dx_rows = jnp.dot(dgate, w_gate.T, preferred_element_type=jnp.float32) + jnp.dot(
            dup, w_up.T, preferred_element_type=jnp.float32
        )
        return out_rows, dx_rows

    def to_send(own):
        rows = own[0].shape[0] // 2
        return jnp.concatenate([a[rows:].astype(jnp.bfloat16) for a in own], axis=1)

    def pair_sums(own, sent):
        size = sent.shape[0] // blocks
        d = own[0].shape[1]
        pieces = []
        for at, to in ((near * size, blocks * size), (0, near * size)):
            got = permute(sent[at:to], core_pairs)
            pieces.append(
                [
                    a[at:to] + got[:, k * d : (k + 1) * d].astype(jnp.float32)
                    for k, a in enumerate(own)
                ]
            )
        return size, pieces[1], pieces[0]

    def block_of(total, part, at):
        size, close, far = total
        if at < near:
            return close[part][at * size : (at + 1) * size]
        return far[part][(at - near) * size : (at - near + 1) * size]

    def wave(total, carry, at):
        if at == 1:
            values = (block_of(total, 1, blocks - 1), block_of(total, 0, blocks - 1))
            values = [v.astype(jnp.bfloat16) for v in values]
        else:
            k = steps - at + 1
            values = []
            for way, index in ((0, 2 * k), (1, 2 * k - 1)):
                out_part, dx_part = (block_of(total, part, index) for part in (0, 1))
                got = carry[way].astype(jnp.float32)
                if at == 2 and way == 0:
                    dx_part = dx_part + got
                elif at == 2:
                    out_part = out_part + got
                else:
                    d = out_part.shape[1]
                    out_part, dx_part = out_part + got[:, :d], dx_part + got[:, d:]
                values.append(
                    jnp.concatenate(
                        [out_part.astype(jnp.bfloat16), dx_part.astype(jnp.bfloat16)], axis=1
                    )
                )
        return lax.optimization_barrier(tuple(values))

    def final(total, carry, part):
        d = total[1][part].shape[1]
        done = block_of(total, part, 0)
        for got in carry:
            done = done + got[:, part * d : (part + 1) * d].astype(jnp.float32)
        return done.astype(jnp.bfloat16)

    def per_device(tokens, out_grad, expert_ids, gate_vals, w_gate, w_up, w_down):
        d = tokens.shape[1]
        wide = d + LANES
        landed = expert_ids == 0
        coef = jnp.sum(jnp.where(landed, gate_vals.astype(jnp.float32), 0.0), axis=1).astype(
            jnp.bfloat16
        )
        routed = jnp.any(landed, axis=1)
        slot = jnp.cumsum(routed.astype(jnp.int32)) - 1
        select = (slot[None, :] == jnp.arange(CAP, dtype=jnp.int32)[:, None]) & routed[None, :]
        select = select.astype(jnp.bfloat16)
        slot_x, slot_dy, slot_coef = (
            jnp.dot(select, a, preferred_element_type=jnp.float32).astype(jnp.bfloat16)
            for a in (tokens, out_grad, coef[:, None])
        )
        slots = jnp.concatenate(
            [slot_x, jnp.broadcast_to(slot_coef, (CAP, LANES)), slot_dy], axis=1
        )
        first_a, first_b = slots[: CAP // 2], slots[CAP // 2 :]

        held_a = both_ways(first_a, first_a)
        first_b, *held_a = lax.optimization_barrier((first_b, *held_a))
        got_a, far_a = gather(first_a, tuple(held_a), wide)
        got_b, far_b = gather(first_b, both_ways(first_b, first_b), wide)
        weights = (w_gate, w_up, w_down)

        rows_a = all_rows(got_a, far_a, early_of(got_a))
        early_b = early_of(got_b)
        sides_a = products(rows_a, wide, *weights)
        out_a, dx_a = rows_of(*sides_a, *weights)
        sent_a = to_send((out_a, dx_a))
        early_b, dx_a, *far_b = lax.optimization_barrier((early_b, dx_a, *far_b))
        total_a = pair_sums((out_a, dx_a), sent_a)
        carry_a = both_ways(*wave(total_a, None, 1))

        rows_b = all_rows(got_b, far_b, early_b)
        hidden_b, dgate_b, dup_b = products(rows_b, wide, *weights)
        dgate_b, *carry_a = lax.optimization_barrier((dgate_b, *carry_a))
        sides_b = (hidden_b, dgate_b, dup_b)
        out_b, dx_b = rows_of(*sides_b, *weights)
        sent_b = to_send((out_b, dx_b))
        carry_a = both_ways(*wave(total_a, carry_a, 2))
        dx_b, *carry_a = lax.optimization_barrier((dx_b, *carry_a))
        total_b = pair_sums((out_b, dx_b), sent_b)

        sides = [jnp.concatenate(pair, axis=0) for pair in zip(sides_a, sides_b)]
        rows = jnp.concatenate([rows_a, rows_b], axis=0)
        hidden, dgate, dup = sides
        work = [(dgate, 0), (dup, 0), (hidden, wide)]
        carry_b = None
        grads, marks = [], []
        for at in range(1, steps + 1):
            if at + 2 <= steps:
                carry_a = both_ways(*wave(total_a, carry_a, at + 2))
            blocks_b = wave(total_b, carry_b, at)
            if work:
                side, offset = work.pop(0)
                side, *blocks_b = lax.optimization_barrier((side, *blocks_b))
                grad, mark = weight_grad(side, rows, offset, d, marks)
                grads.append(grad)
                carry_b = both_ways(*blocks_b)
                if work and at < steps:
                    mark, *carry_b = lax.optimization_barrier((mark, *carry_b))
                marks = [mark]
            else:
                carry_b = both_ways(*blocks_b)
        for side, offset in work:
            grads.append(weight_grad(side, rows, offset, d, marks)[0])
        grad_gate, grad_up, grad_down = grads
        mixed, grad_tokens = (
            jnp.dot(
                select.T,
                jnp.concatenate(
                    [final(total_a, carry_a, part), final(total_b, carry_b, part)], axis=0
                ),
                preferred_element_type=jnp.float32,
            ).astype(jnp.bfloat16)
            for part in (0, 1)
        )
        return (mixed, grad_tokens, grad_gate.T, grad_up.T, grad_down)

    return per_device


def solution(mesh):
    placed = (
        P(("groups", "et"), None),
        P(("groups", "et"), None),
        P(("groups", "et"), None),
        P(("groups", "et"), None),
        P(None, "et"),
        P(None, "et"),
        P("et", None),
    )
    return jax.shard_map(
        make_per_device(mesh.shape["et"]),
        mesh=mesh,
        in_specs=placed,
        out_specs=(
            P(("groups", "et"), None),
            P(("groups", "et"), None),
            P("groups", "et"),
            P("groups", "et"),
            P(("groups", "et"), None),
        ),
        check_vma=False,
    )
```

```python
import jax
import jax.numpy as jnp
from jax import lax
from jax.experimental import pallas as pl
from jax.experimental.pallas import tpu as pltpu
from jax.sharding import PartitionSpec as P

CAP = 16
LANES = 128
ANY = pl.BlockSpec(memory_space=pl.ANY)
MARK = jax.ShapeDtypeStruct((8, LANES), jnp.float32)


def parts_of(d, most):
    width = LANES
    for w in range(LANES, most + 1, LANES):
        if d % w == 0:
            width = w
    return d // width, width


def params(megabytes):
    return pltpu.CompilerParams(vmem_limit_bytes=megabytes << 20)


def grad_kernel(parts, width, marks, side_ref, rows_ref, *refs):
    out_ref, mark_ref, rows_buf, out_buf, load_sem, store_sem = refs[marks:]
    spans = [pl.ds(j * width, width) for j in range(parts)]
    loads = [
        pltpu.make_async_copy(rows_ref.at[:, at], rows_buf.at[:, at], load_sem.at[j])
        for j, at in enumerate(spans)
    ]
    stores = [
        pltpu.make_async_copy(out_buf.at[:, at], out_ref.at[:, at], store_sem.at[j])
        for j, at in enumerate(spans)
    ]
    for load in loads:
        load.start()
    mark_ref[...] = jnp.zeros(mark_ref.shape, jnp.float32)
    side = side_ref[...]
    for j, at in enumerate(spans):
        loads[j].wait()
        out_buf[:, at] = jnp.dot(
            side, rows_buf[:, at], preferred_element_type=jnp.float32
        ).astype(jnp.bfloat16)
        stores[j].start()
    for store in stores:
        store.wait()


def weight_grad(side, rows, d, marks):
    r, f = side.shape
    parts, width = parts_of(d, 1024)
    return pl.pallas_call(
        lambda *refs: grad_kernel(parts, width, len(marks), *refs),
        in_specs=[pl.BlockSpec(memory_space=pltpu.VMEM), ANY] + [ANY] * len(marks),
        out_specs=[ANY, pl.BlockSpec(memory_space=pltpu.VMEM)],
        out_shape=[jax.ShapeDtypeStruct((f, d), jnp.bfloat16), MARK],
        scratch_shapes=[
            pltpu.VMEM((r, d), jnp.bfloat16),
            pltpu.VMEM((f, d), jnp.bfloat16),
            pltpu.SemaphoreType.DMA((parts,)),
            pltpu.SemaphoreType.DMA((parts,)),
        ],
        compiler_params=params(20),
        cost_estimate=pl.CostEstimate(
            flops=2 * r * f * d, bytes_accessed=2 * d * (r + f), transcendentals=0
        ),
    )(side.T, rows, *marks)


def ring_of(n):
    chips = n // 2
    order = list(range(0, chips, 2)) + list(range(chips - 1, 0, -2))
    right = []
    for at, chip in enumerate(order):
        nxt = order[(at + 1) % chips]
        right += [(2 * chip + core, 2 * nxt + core) for core in (0, 1)]
    return right, [(b, a) for a, b in right]


def make_per_device(n):
    steps = n // 4
    core_pairs = [(i, i ^ 1) for i in range(n)]
    right_pairs, left_pairs = ring_of(n)

    def permute(x, pairs):
        return lax.ppermute(x, "et", pairs)

    def far_block(held_r, held_l):
        at = held_r.shape[1] // 2 // LANES * LANES
        return jnp.concatenate(
            [permute(held_r[:, :at], right_pairs), permute(held_l[:, at:], left_pairs)], axis=1
        )

    def gather_rows(x, dy):
        held_xr = held_xl = x
        held_dr = held_dl = dy
        got_x, got_d = [x], [dy]
        for k in range(1, steps):
            held_xr = permute(held_xr, right_pairs)
            held_xl = permute(held_xl, left_pairs)
            held_dr = permute(held_dr, right_pairs)
            held_dl = permute(held_dl, left_pairs)
            got_x += [held_xr, held_xl]
            got_d += [held_dr, held_dl]
        got_d.append(far_block(held_dr, held_dl))
        far_x = far_block(held_xr, held_xl)
        early_x = permute(jnp.concatenate(got_x, axis=0), core_pairs)
        late_x = permute(far_x, core_pairs)
        chip_d, late_x = lax.optimization_barrier((jnp.concatenate(got_d, axis=0), late_x))
        rows_x = jnp.concatenate(got_x + [far_x, early_x, late_x], axis=0)
        return rows_x, jnp.concatenate(got_d + [permute(chip_d, core_pairs)], axis=0)

    cut = max(2 * steps - 3, 1) * CAP

    def pair_sum(own, sent):
        far = own[cut:] + permute(sent[cut:], core_pairs).astype(jnp.float32)
        near = own[:cut] + permute(sent[:cut], core_pairs).astype(jnp.float32)
        return near, far

    def block_of(total, at):
        at = at * CAP
        return total[0][at : at + CAP] if at < cut else total[1][at - cut : at - cut + CAP]

    def wave(total, carry, at, far_way):
        blocks = {}
        for way in ("l", "r"):
            k = steps - at + (way == far_way)
            if k < 1:
                continue
            block = block_of(total, 2 * k - (way == "l" or k == steps))
            if way in carry:
                block = block + carry[way].astype(jnp.float32)
            blocks[way] = block.astype(jnp.bfloat16)
        return lax.optimization_barrier(blocks)

    def send(blocks):
        return {w: permute(b, left_pairs if w == "l" else right_pairs) for w, b in blocks.items()}

    def final(near, carry):
        done = near[:CAP] + carry["l"].astype(jnp.float32) + carry["r"].astype(jnp.float32)
        return done.astype(jnp.bfloat16)

    def tie(value, blocks):
        ways = list(blocks)
        tied = lax.optimization_barrier((value, *[blocks[w] for w in ways]))
        return tied[0], dict(zip(ways, tied[1:]))

    def per_device(tokens, out_grad, expert_ids, gate_vals, w_gate, w_up, w_down):
        d = tokens.shape[1]
        landed = expert_ids == 0
        coef = jnp.sum(jnp.where(landed, gate_vals.astype(jnp.float32), 0.0), axis=1).astype(
            jnp.bfloat16
        )
        routed = jnp.any(landed, axis=1)
        slot = jnp.cumsum(routed.astype(jnp.int32)) - 1
        select = (slot[None, :] == jnp.arange(CAP, dtype=jnp.int32)[:, None]) & routed[None, :]
        select = select.astype(jnp.bfloat16)
        slot_x, slot_dy, slot_coef = (
            jnp.dot(select, a, preferred_element_type=jnp.float32).astype(jnp.bfloat16)
            for a in (tokens, out_grad, coef[:, None])
        )
        slot_coef = jnp.broadcast_to(slot_coef, (CAP, LANES))
        rows_wide, rows_dy = gather_rows(
            jnp.concatenate([slot_x, slot_coef], axis=1), slot_dy
        )
        rows_x = rows_wide[:, :d]
        coef_rows = rows_wide[:, d : d + 1].astype(jnp.float32)
        half = rows_wide.shape[0] // 2

        gate = jnp.dot(rows_x, w_gate, preferred_element_type=jnp.float32)
        up = jnp.dot(rows_x, w_up, preferred_element_type=jnp.float32)
        sig = jax.nn.sigmoid(gate)
        act = gate * sig
        hidden = (coef_rows * act * up).astype(jnp.bfloat16)
        out_rows = jnp.dot(hidden, w_down, preferred_element_type=jnp.float32)
        out_sent = out_rows[half:].astype(jnp.bfloat16)
        rows_dy, out_sent = lax.optimization_barrier((rows_dy, out_sent))
        out_total = pair_sum(out_rows[:half], out_sent)

        dhid = jnp.dot(rows_dy, w_down.T, preferred_element_type=jnp.float32)
        scaled = coef_rows * dhid
        dgate = (scaled * up * sig * (1.0 + gate * (1.0 - sig))).astype(jnp.bfloat16)
        dup = (scaled * act).astype(jnp.bfloat16)
        dgate, blocks = tie(dgate, wave(out_total, {}, 1, "l"))
        out_carry = send(blocks)
        dx_rows = jnp.dot(dgate, w_gate.T, preferred_element_type=jnp.float32) + jnp.dot(
            dup, w_up.T, preferred_element_type=jnp.float32
        )
        dx_sent = dx_rows[half:].astype(jnp.bfloat16)
        hidden, dx_sent = lax.optimization_barrier((hidden, dx_sent))
        grad_down, mark = weight_grad(hidden, rows_dy, d, [])
        mark, out_carry = tie(mark, out_carry)
        dx_total = pair_sum(dx_rows[:half], dx_sent)
        dx_carry = {}

        grads, marks = [], [mark]
        work = [dgate, dup]
        for at in range(2, steps + 2):
            if at <= steps:
                out_carry.update(send(wave(out_total, out_carry, at, "l")))
            dx_blocks = wave(dx_total, dx_carry, at - 1, "r")
            if work:
                side, dx_blocks = tie(work.pop(0), dx_blocks)
                grad, mark = weight_grad(side, rows_wide, d, marks)
                grads.append(grad)
                if work and at <= steps:
                    mark, out_carry = tie(mark, out_carry)
                marks = [mark]
            dx_carry.update(send(dx_blocks))
        for side in work:
            grads.append(weight_grad(side, rows_wide, d, marks)[0])
        grad_gate, grad_up = grads
        mixed, grad_tokens = (
            jnp.dot(select.T, final(total[0], carry), preferred_element_type=jnp.float32).astype(
                jnp.bfloat16
            )
            for total, carry in ((out_total, out_carry), (dx_total, dx_carry))
        )
        return (mixed, grad_tokens, grad_gate.T, grad_up.T, grad_down)

    return per_device


def solution(mesh):
    placed = (
        P(("groups", "et"), None),
        P(("groups", "et"), None),
        P(("groups", "et"), None),
        P(("groups", "et"), None),
        P(None, "et"),
        P(None, "et"),
        P("et", None),
    )
    return jax.shard_map(
        make_per_device(mesh.shape["et"]),
        mesh=mesh,
        in_specs=placed,
        out_specs=(
            P(("groups", "et"), None),
            P(("groups", "et"), None),
            P("groups", "et"),
            P("groups", "et"),
            P(("groups", "et"), None),
        ),
        check_vma=False,
    )
```

```python
import jax
import jax.numpy as jnp
from jax import lax
from jax.experimental import pallas as pl
from jax.experimental.pallas import tpu as pltpu
from jax.sharding import PartitionSpec as P

CAP = 16
LANES = 128
ANY = pl.BlockSpec(memory_space=pl.ANY)
MARK = jax.ShapeDtypeStruct((8, LANES), jnp.float32)


def parts_of(d, most):
    width = LANES
    for w in range(LANES, most + 1, LANES):
        if d % w == 0:
            width = w
    return d // width, width


def params(megabytes):
    return pltpu.CompilerParams(vmem_limit_bytes=megabytes << 20)


def grad_kernel(parts, width, marks, side_ref, rows_ref, *refs):
    out_ref, mark_ref, rows_buf, out_buf, load_sem, store_sem = refs[marks:]
    spans = [pl.ds(j * width, width) for j in range(parts)]
    loads = [
        pltpu.make_async_copy(rows_ref.at[:, at], rows_buf.at[:, at], load_sem.at[j])
        for j, at in enumerate(spans)
    ]
    stores = [
        pltpu.make_async_copy(out_buf.at[:, at], out_ref.at[:, at], store_sem.at[j])
        for j, at in enumerate(spans)
    ]
    for load in loads:
        load.start()
    mark_ref[...] = jnp.zeros(mark_ref.shape, jnp.float32)
    side = side_ref[...]
    for j, at in enumerate(spans):
        loads[j].wait()
        out_buf[:, at] = jnp.dot(
            side, rows_buf[:, at], preferred_element_type=jnp.float32
        ).astype(jnp.bfloat16)
        stores[j].start()
    for store in stores:
        store.wait()


def weight_grad(side, rows, d, marks):
    r, f = side.shape
    parts, width = parts_of(d, 1024)
    return pl.pallas_call(
        lambda *refs: grad_kernel(parts, width, len(marks), *refs),
        in_specs=[pl.BlockSpec(memory_space=pltpu.VMEM), ANY] + [ANY] * len(marks),
        out_specs=[ANY, pl.BlockSpec(memory_space=pltpu.VMEM)],
        out_shape=[jax.ShapeDtypeStruct((f, d), jnp.bfloat16), MARK],
        scratch_shapes=[
            pltpu.VMEM((r, d), jnp.bfloat16),
            pltpu.VMEM((f, d), jnp.bfloat16),
            pltpu.SemaphoreType.DMA((parts,)),
            pltpu.SemaphoreType.DMA((parts,)),
        ],
        compiler_params=params(20),
        cost_estimate=pl.CostEstimate(
            flops=2 * r * f * d, bytes_accessed=2 * d * (r + f), transcendentals=0
        ),
    )(side.T, rows, *marks)


def ring_of(n):
    chips = n // 2
    order = list(range(0, chips, 2)) + list(range(chips - 1, 0, -2))
    right = []
    for at, chip in enumerate(order):
        nxt = order[(at + 1) % chips]
        right += [(2 * chip + core, 2 * nxt + core) for core in (0, 1)]
    return right, [(b, a) for a, b in right]


def make_per_device(n):
    steps = n // 4
    core_pairs = [(i, i ^ 1) for i in range(n)]
    right_pairs, left_pairs = ring_of(n)

    def permute(x, pairs):
        return lax.ppermute(x, "et", pairs)

    def far_block(held_r, held_l):
        at = held_r.shape[1] // 2 // LANES * LANES
        return jnp.concatenate(
            [permute(held_r[:, :at], right_pairs), permute(held_l[:, at:], left_pairs)], axis=1
        )

    def gather_rows(x, dy):
        held_xr = held_xl = x
        held_dr = held_dl = dy
        got_x, got_d = [x], [dy]
        for k in range(1, steps):
            held_xr = permute(held_xr, right_pairs)
            held_xl = permute(held_xl, left_pairs)
            held_dr = permute(held_dr, right_pairs)
            held_dl = permute(held_dl, left_pairs)
            got_x += [held_xr, held_xl]
            got_d += [held_dr, held_dl]
        got_d.append(far_block(held_dr, held_dl))
        far_x = far_block(held_xr, held_xl)
        early_x = permute(jnp.concatenate(got_x, axis=0), core_pairs)
        late_x = permute(far_x, core_pairs)
        chip_d, late_x = lax.optimization_barrier((jnp.concatenate(got_d, axis=0), late_x))
        rows_x = jnp.concatenate(got_x + [far_x, early_x, late_x], axis=0)
        return rows_x, jnp.concatenate(got_d + [permute(chip_d, core_pairs)], axis=0)

    cut = max(2 * steps - 3, 1) * CAP

    def pair_sum(own, sent):
        far = own[cut:] + permute(sent[cut:], core_pairs).astype(jnp.float32)
        near = own[:cut] + permute(sent[:cut], core_pairs).astype(jnp.float32)
        return near, far

    def block_of(total, at):
        at = at * CAP
        return total[0][at : at + CAP] if at < cut else total[1][at - cut : at - cut + CAP]

    def wave(total, carry, at, far_way):
        blocks = {}
        for way in ("l", "r"):
            k = steps - at + (way == far_way)
            if k < 1:
                continue
            block = block_of(total, 2 * k - (way == "l" or k == steps))
            if way in carry:
                block = block + carry[way].astype(jnp.float32)
            blocks[way] = block.astype(jnp.bfloat16)
        return lax.optimization_barrier(blocks)

    def send(blocks):
        return {w: permute(b, left_pairs if w == "l" else right_pairs) for w, b in blocks.items()}

    def final(near, carry):
        done = near[:CAP] + carry["l"].astype(jnp.float32) + carry["r"].astype(jnp.float32)
        return done.astype(jnp.bfloat16)

    def tie(value, blocks):
        ways = list(blocks)
        tied = lax.optimization_barrier((value, *[blocks[w] for w in ways]))
        return tied[0], dict(zip(ways, tied[1:]))

    def per_device(tokens, out_grad, expert_ids, gate_vals, w_gate, w_up, w_down):
        d = tokens.shape[1]
        landed = expert_ids == 0
        coef = jnp.sum(jnp.where(landed, gate_vals.astype(jnp.float32), 0.0), axis=1).astype(
            jnp.bfloat16
        )
        routed = jnp.any(landed, axis=1)
        slot = jnp.cumsum(routed.astype(jnp.int32)) - 1
        select = (slot[None, :] == jnp.arange(CAP, dtype=jnp.int32)[:, None]) & routed[None, :]
        select = select.astype(jnp.bfloat16)
        slot_x, slot_dy, slot_coef = (
            jnp.dot(select, a, preferred_element_type=jnp.float32).astype(jnp.bfloat16)
            for a in (tokens, out_grad, coef[:, None])
        )
        slot_coef = jnp.broadcast_to(slot_coef, (CAP, LANES))
        rows_wide, rows_dy = gather_rows(
            jnp.concatenate([slot_x, slot_coef], axis=1), slot_dy
        )
        rows_x = rows_wide[:, :d]
        coef_rows = rows_wide[:, d : d + 1].astype(jnp.float32)
        half = rows_wide.shape[0] // 2

        gate = jnp.dot(rows_x, w_gate, preferred_element_type=jnp.float32)
        up = jnp.dot(rows_x, w_up, preferred_element_type=jnp.float32)
        sig = jax.nn.sigmoid(gate)
        act = gate * sig
        hidden = (coef_rows * act * up).astype(jnp.bfloat16)
        out_rows = jnp.dot(hidden, w_down, preferred_element_type=jnp.float32)
        out_sent = out_rows[half:].astype(jnp.bfloat16)
        rows_dy, out_sent = lax.optimization_barrier((rows_dy, out_sent))
        out_total = pair_sum(out_rows[:half], out_sent)

        dhid = jnp.dot(rows_dy, w_down.T, preferred_element_type=jnp.float32)
        scaled = coef_rows * dhid
        dgate = (scaled * up * sig * (1.0 + gate * (1.0 - sig))).astype(jnp.bfloat16)
        dup = (scaled * act).astype(jnp.bfloat16)
        dgate, blocks = tie(dgate, wave(out_total, {}, 1, "l"))
        out_carry = send(blocks)
        dx_rows = jnp.dot(dgate, w_gate.T, preferred_element_type=jnp.float32) + jnp.dot(
            dup, w_up.T, preferred_element_type=jnp.float32
        )
        dx_sent = dx_rows[half:].astype(jnp.bfloat16)
        dx_sent, out_carry = tie(dx_sent, out_carry)
        dx_total = pair_sum(dx_rows[:half], dx_sent)
        dx_carry = {}

        grads, marks = [], []
        work = [(dgate, rows_wide), (dup, rows_wide), (hidden, rows_dy)]
        for at in range(2, steps + 2):
            if at <= steps:
                out_carry.update(send(wave(out_total, out_carry, at, "l")))
            dx_blocks = wave(dx_total, dx_carry, at - 1, "r")
            if work:
                side, rows = work.pop(0)
                side, dx_blocks = tie(side, dx_blocks)
                grad, mark = weight_grad(side, rows, d, marks)
                grads.append(grad)
                if work and at <= steps:
                    mark, out_carry = tie(mark, out_carry)
                marks = [mark]
            dx_carry.update(send(dx_blocks))
        for side, rows in work:
            grads.append(weight_grad(side, rows, d, marks)[0])
        grad_gate, grad_up, grad_down = grads
        mixed, grad_tokens = (
            jnp.dot(select.T, final(total[0], carry), preferred_element_type=jnp.float32).astype(
                jnp.bfloat16
            )
            for total, carry in ((out_total, out_carry), (dx_total, dx_carry))
        )
        return (mixed, grad_tokens, grad_gate.T, grad_up.T, grad_down)

    return per_device


def solution(mesh):
    placed = (
        P(("groups", "et"), None),
        P(("groups", "et"), None),
        P(("groups", "et"), None),
        P(("groups", "et"), None),
        P(None, "et"),
        P(None, "et"),
        P("et", None),
    )
    return jax.shard_map(
        make_per_device(mesh.shape["et"]),
        mesh=mesh,
        in_specs=placed,
        out_specs=(
            P(("groups", "et"), None),
            P(("groups", "et"), None),
            P("groups", "et"),
            P("groups", "et"),
            P(("groups", "et"), None),
        ),
        check_vma=False,
    )
```

```python
import jax
import jax.numpy as jnp
from jax import lax
from jax.experimental import pallas as pl
from jax.experimental.pallas import tpu as pltpu
from jax.sharding import PartitionSpec as P

CAP = 16
LANES = 128
ANY = pl.BlockSpec(memory_space=pl.ANY)
MARK = jax.ShapeDtypeStruct((8, LANES), jnp.float32)


def parts_of(d, most):
    width = LANES
    for w in range(LANES, most + 1, LANES):
        if d % w == 0:
            width = w
    return d // width, width


def params(megabytes):
    return pltpu.CompilerParams(vmem_limit_bytes=megabytes << 20)


def grad_kernel(parts, width, marks, side_ref, rows_ref, *refs):
    out_ref, mark_ref, rows_buf, out_buf, load_sem, store_sem = refs[marks:]
    spans = [pl.ds(j * width, width) for j in range(parts)]
    loads = [
        pltpu.make_async_copy(rows_ref.at[:, at], rows_buf.at[:, at], load_sem.at[j])
        for j, at in enumerate(spans)
    ]
    stores = [
        pltpu.make_async_copy(out_buf.at[:, at], out_ref.at[:, at], store_sem.at[j])
        for j, at in enumerate(spans)
    ]
    for load in loads:
        load.start()
    mark_ref[...] = jnp.zeros(mark_ref.shape, jnp.float32)
    side = side_ref[...]
    for j, at in enumerate(spans):
        loads[j].wait()
        out_buf[:, at] = jnp.dot(
            side, rows_buf[:, at], preferred_element_type=jnp.float32
        ).astype(jnp.bfloat16)
        stores[j].start()
    for store in stores:
        store.wait()


def weight_grad(side, rows, d, marks):
    r, f = side.shape
    parts, width = parts_of(d, 1024)
    return pl.pallas_call(
        lambda *refs: grad_kernel(parts, width, len(marks), *refs),
        in_specs=[pl.BlockSpec(memory_space=pltpu.VMEM), ANY] + [ANY] * len(marks),
        out_specs=[ANY, pl.BlockSpec(memory_space=pltpu.VMEM)],
        out_shape=[jax.ShapeDtypeStruct((f, d), jnp.bfloat16), MARK],
        scratch_shapes=[
            pltpu.VMEM((r, d), jnp.bfloat16),
            pltpu.VMEM((f, d), jnp.bfloat16),
            pltpu.SemaphoreType.DMA((parts,)),
            pltpu.SemaphoreType.DMA((parts,)),
        ],
        compiler_params=params(20),
        cost_estimate=pl.CostEstimate(
            flops=2 * r * f * d, bytes_accessed=2 * d * (r + f), transcendentals=0
        ),
    )(side.T, rows, *marks)


def ring_of(n):
    chips = n // 2
    order = list(range(0, chips, 2)) + list(range(chips - 1, 0, -2))
    right = []
    for at, chip in enumerate(order):
        nxt = order[(at + 1) % chips]
        right += [(2 * chip + core, 2 * nxt + core) for core in (0, 1)]
    return right, [(b, a) for a, b in right]


def make_per_device(n):
    steps = n // 4
    core_pairs = [(i, i ^ 1) for i in range(n)]
    right_pairs, left_pairs = ring_of(n)

    def permute(x, pairs):
        return lax.ppermute(x, "et", pairs)

    def far_block(held_r, held_l):
        at = held_r.shape[1] // 2 // LANES * LANES
        return jnp.concatenate(
            [permute(held_r[:, :at], right_pairs), permute(held_l[:, at:], left_pairs)], axis=1
        )

    def gather_rows(x, dy):
        held_xr = held_xl = x
        held_dr = held_dl = dy
        got_x, got_d = [x], [dy]
        for k in range(1, steps):
            held_xr = permute(held_xr, right_pairs)
            held_xl = permute(held_xl, left_pairs)
            held_dr = permute(held_dr, right_pairs)
            held_dl = permute(held_dl, left_pairs)
            got_x += [held_xr, held_xl]
            got_d += [held_dr, held_dl]
        got_d.append(far_block(held_dr, held_dl))
        far_x = far_block(held_xr, held_xl)
        early_x = permute(jnp.concatenate(got_x, axis=0), core_pairs)
        late_x = permute(far_x, core_pairs)
        chip_d, late_x = lax.optimization_barrier((jnp.concatenate(got_d, axis=0), late_x))
        rows_x = jnp.concatenate(got_x + [far_x, early_x, late_x], axis=0)
        return rows_x, jnp.concatenate(got_d + [permute(chip_d, core_pairs)], axis=0)

    cut = max(2 * steps - 3, 1) * CAP

    def pair_sum(own, sent):
        far = own[cut:] + permute(sent[cut:], core_pairs).astype(jnp.float32)
        near = own[:cut] + permute(sent[:cut], core_pairs).astype(jnp.float32)
        return near, far

    def block_of(total, at):
        at = at * CAP
        return total[0][at : at + CAP] if at < cut else total[1][at - cut : at - cut + CAP]

    def wave(total, carry, at, far_way):
        blocks = {}
        for way in ("l", "r"):
            k = steps - at + (way == far_way)
            if k < 1:
                continue
            block = block_of(total, 2 * k - (way == "l" or k == steps))
            if way in carry:
                block = block + carry[way].astype(jnp.float32)
            blocks[way] = block.astype(jnp.bfloat16)
        return lax.optimization_barrier(blocks)

    def send(blocks):
        return {w: permute(b, left_pairs if w == "l" else right_pairs) for w, b in blocks.items()}

    def final(near, carry):
        done = near[:CAP] + carry["l"].astype(jnp.float32) + carry["r"].astype(jnp.float32)
        return done.astype(jnp.bfloat16)

    def tie(value, blocks):
        ways = list(blocks)
        tied = lax.optimization_barrier((value, *[blocks[w] for w in ways]))
        return tied[0], dict(zip(ways, tied[1:]))

    def per_device(tokens, out_grad, expert_ids, gate_vals, w_gate, w_up, w_down):
        d = tokens.shape[1]
        landed = expert_ids == 0
        coef = jnp.sum(jnp.where(landed, gate_vals.astype(jnp.float32), 0.0), axis=1).astype(
            jnp.bfloat16
        )
        routed = jnp.any(landed, axis=1)
        slot = jnp.cumsum(routed.astype(jnp.int32)) - 1
        select = (slot[None, :] == jnp.arange(CAP, dtype=jnp.int32)[:, None]) & routed[None, :]
        select = select.astype(jnp.bfloat16)
        slot_x, slot_dy, slot_coef = (
            jnp.dot(select, a, preferred_element_type=jnp.float32).astype(jnp.bfloat16)
            for a in (tokens, out_grad, coef[:, None])
        )
        slot_coef = jnp.broadcast_to(slot_coef, (CAP, LANES))
        rows_wide, rows_dy = gather_rows(
            jnp.concatenate([slot_x, slot_coef], axis=1), slot_dy
        )
        rows_x = rows_wide[:, :d]
        coef_rows = rows_wide[:, d : d + 1].astype(jnp.float32)
        half = rows_wide.shape[0] // 2

        gate = jnp.dot(rows_x, w_gate, preferred_element_type=jnp.float32)
        up = jnp.dot(rows_x, w_up, preferred_element_type=jnp.float32)
        sig = jax.nn.sigmoid(gate)
        act = gate * sig
        hidden = (coef_rows * act * up).astype(jnp.bfloat16)
        out_rows = jnp.dot(hidden, w_down, preferred_element_type=jnp.float32)
        out_sent = out_rows[half:].astype(jnp.bfloat16)
        rows_dy, out_sent = lax.optimization_barrier((rows_dy, out_sent))
        out_total = pair_sum(out_rows[:half], out_sent)

        dhid = jnp.dot(rows_dy, w_down.T, preferred_element_type=jnp.float32)
        scaled = coef_rows * dhid
        dgate = (scaled * up * sig * (1.0 + gate * (1.0 - sig))).astype(jnp.bfloat16)
        dup = (scaled * act).astype(jnp.bfloat16)
        dgate, blocks = tie(dgate, wave(out_total, {}, 1, "l"))
        out_carry = send(blocks)
        dx_rows = jnp.dot(dgate, w_gate.T, preferred_element_type=jnp.float32) + jnp.dot(
            dup, w_up.T, preferred_element_type=jnp.float32
        )
        dx_sent = dx_rows[half:].astype(jnp.bfloat16)
        dx_total = pair_sum(dx_rows[:half], dx_sent)
        dx_carry = {}

        grads = []
        work = [(hidden, rows_dy), (dgate, rows_wide), (dup, rows_wide)]
        for at in range(1, steps + 1):
            if at > 1:
                out_carry.update(send(wave(out_total, out_carry, at, "l")))
            dx_blocks = wave(dx_total, dx_carry, at, "r")
            if work:
                side, rows = work.pop(0)
                side, dx_blocks = tie(side, dx_blocks)
                grad, mark = weight_grad(side, rows, d, [])
                grads.append(grad)
                zero = mark[0, 0].astype(jnp.bfloat16)
                out_carry = {w: c + zero for w, c in out_carry.items()}
            dx_carry.update(send(dx_blocks))
        for side, rows in work:
            grads.append(weight_grad(side, rows, d, [])[0])
        grad_down, grad_gate, grad_up = grads
        mixed, grad_tokens = (
            jnp.dot(select.T, final(total[0], carry), preferred_element_type=jnp.float32).astype(
                jnp.bfloat16
            )
            for total, carry in ((out_total, out_carry), (dx_total, dx_carry))
        )
        return (mixed, grad_tokens, grad_gate.T, grad_up.T, grad_down)

    return per_device


def solution(mesh):
    placed = (
        P(("groups", "et"), None),
        P(("groups", "et"), None),
        P(("groups", "et"), None),
        P(("groups", "et"), None),
        P(None, "et"),
        P(None, "et"),
        P("et", None),
    )
    return jax.shard_map(
        make_per_device(mesh.shape["et"]),
        mesh=mesh,
        in_specs=placed,
        out_specs=(
            P(("groups", "et"), None),
            P(("groups", "et"), None),
            P("groups", "et"),
            P("groups", "et"),
            P(("groups", "et"), None),
        ),
        check_vma=False,
    )
```

```python
import jax
import jax.numpy as jnp
from jax import lax
from jax.experimental import pallas as pl
from jax.experimental.pallas import tpu as pltpu
from jax.sharding import PartitionSpec as P

CAP = 16
LANES = 128
ANY = pl.BlockSpec(memory_space=pl.ANY)
MARK = jax.ShapeDtypeStruct((8, LANES), jnp.float32)


def parts_of(d, most):
    width = LANES
    for w in range(LANES, most + 1, LANES):
        if d % w == 0:
            width = w
    return d // width, width


def params(megabytes):
    return pltpu.CompilerParams(vmem_limit_bytes=megabytes << 20)


def grad_kernel(parts, width, marks, side_ref, rows_ref, *refs):
    out_ref, mark_ref, rows_buf, out_buf, load_sem, store_sem = refs[marks:]
    spans = [pl.ds(j * width, width) for j in range(parts)]
    loads = [
        pltpu.make_async_copy(rows_ref.at[:, at], rows_buf.at[:, at], load_sem.at[j])
        for j, at in enumerate(spans)
    ]
    stores = [
        pltpu.make_async_copy(out_buf.at[:, at], out_ref.at[:, at], store_sem.at[j])
        for j, at in enumerate(spans)
    ]
    for load in loads:
        load.start()
    mark_ref[...] = jnp.zeros(mark_ref.shape, jnp.float32)
    side = side_ref[...]
    for j, at in enumerate(spans):
        loads[j].wait()
        out_buf[:, at] = jnp.dot(
            side, rows_buf[:, at], preferred_element_type=jnp.float32
        ).astype(jnp.bfloat16)
        stores[j].start()
    for store in stores:
        store.wait()


def weight_grad(side, rows, d, marks):
    r, f = side.shape
    parts, width = parts_of(d, 1024)
    return pl.pallas_call(
        lambda *refs: grad_kernel(parts, width, len(marks), *refs),
        in_specs=[pl.BlockSpec(memory_space=pltpu.VMEM), ANY] + [ANY] * len(marks),
        out_specs=[ANY, pl.BlockSpec(memory_space=pltpu.VMEM)],
        out_shape=[jax.ShapeDtypeStruct((f, d), jnp.bfloat16), MARK],
        scratch_shapes=[
            pltpu.VMEM((r, d), jnp.bfloat16),
            pltpu.VMEM((f, d), jnp.bfloat16),
            pltpu.SemaphoreType.DMA((parts,)),
            pltpu.SemaphoreType.DMA((parts,)),
        ],
        compiler_params=params(20),
        cost_estimate=pl.CostEstimate(
            flops=2 * r * f * d, bytes_accessed=2 * d * (r + f), transcendentals=0
        ),
    )(side.T, rows, *marks)


def ring_of(n):
    chips = n // 2
    order = list(range(0, chips, 2)) + list(range(chips - 1, 0, -2))
    right = []
    for at, chip in enumerate(order):
        nxt = order[(at + 1) % chips]
        right += [(2 * chip + core, 2 * nxt + core) for core in (0, 1)]
    return right, [(b, a) for a, b in right]


def make_per_device(n):
    steps = n // 4
    core_pairs = [(i, i ^ 1) for i in range(n)]
    right_pairs, left_pairs = ring_of(n)

    def permute(x, pairs):
        return lax.ppermute(x, "et", pairs)

    def far_block(held_r, held_l):
        at = held_r.shape[1] // 2 // LANES * LANES
        return jnp.concatenate(
            [permute(held_r[:, :at], right_pairs), permute(held_l[:, at:], left_pairs)], axis=1
        )

    def gather_rows(x, dy):
        held_xr = held_xl = x
        held_dr = held_dl = dy
        got_x, got_d = [x], [dy]
        for k in range(1, steps):
            held_xr = permute(held_xr, right_pairs)
            held_xl = permute(held_xl, left_pairs)
            held_dr = permute(held_dr, right_pairs)
            held_dl = permute(held_dl, left_pairs)
            got_x += [held_xr, held_xl]
            got_d += [held_dr, held_dl]
        got_d.append(far_block(held_dr, held_dl))
        far_x = far_block(held_xr, held_xl)
        early_x = permute(jnp.concatenate(got_x, axis=0), core_pairs)
        late_x = permute(far_x, core_pairs)
        chip_d, late_x = lax.optimization_barrier((jnp.concatenate(got_d, axis=0), late_x))
        rows_x = jnp.concatenate(got_x + [far_x, early_x, late_x], axis=0)
        return rows_x, jnp.concatenate(got_d + [permute(chip_d, core_pairs)], axis=0)

    cut = max(2 * steps - 3, 1) * CAP

    def pair_sum(own, sent):
        far = own[cut:] + permute(sent[cut:], core_pairs).astype(jnp.float32)
        near = own[:cut] + permute(sent[:cut], core_pairs).astype(jnp.float32)
        return near, far

    def block_of(total, at):
        at = at * CAP
        return total[0][at : at + CAP] if at < cut else total[1][at - cut : at - cut + CAP]

    def wave(total, carry, at, far_way):
        blocks = {}
        for way in ("l", "r"):
            k = steps - at + (way == far_way)
            if k < 1:
                continue
            block = block_of(total, 2 * k - (way == "l" or k == steps))
            if way in carry:
                block = block + carry[way].astype(jnp.float32)
            blocks[way] = block.astype(jnp.bfloat16)
        return lax.optimization_barrier(blocks)

    def send(blocks):
        return {w: permute(b, left_pairs if w == "l" else right_pairs) for w, b in blocks.items()}

    def final(near, carry):
        done = near[:CAP] + carry["l"].astype(jnp.float32) + carry["r"].astype(jnp.float32)
        return done.astype(jnp.bfloat16)

    def tie(value, blocks):
        ways = list(blocks)
        tied = lax.optimization_barrier((value, *[blocks[w] for w in ways]))
        return tied[0], dict(zip(ways, tied[1:]))

    def per_device(tokens, out_grad, expert_ids, gate_vals, w_gate, w_up, w_down):
        d = tokens.shape[1]
        landed = expert_ids == 0
        coef = jnp.sum(jnp.where(landed, gate_vals.astype(jnp.float32), 0.0), axis=1).astype(
            jnp.bfloat16
        )
        routed = jnp.any(landed, axis=1)
        slot = jnp.cumsum(routed.astype(jnp.int32)) - 1
        select = (slot[None, :] == jnp.arange(CAP, dtype=jnp.int32)[:, None]) & routed[None, :]
        select = select.astype(jnp.bfloat16)
        slot_x, slot_dy, slot_coef = (
            jnp.dot(select, a, preferred_element_type=jnp.float32).astype(jnp.bfloat16)
            for a in (tokens, out_grad, coef[:, None])
        )
        slot_coef = jnp.broadcast_to(slot_coef, (CAP, LANES))
        rows_wide, rows_dy = gather_rows(
            jnp.concatenate([slot_x, slot_coef], axis=1), slot_dy
        )
        rows_x = rows_wide[:, :d]
        coef_rows = rows_wide[:, d : d + 1].astype(jnp.float32)
        half = rows_wide.shape[0] // 2

        gate = jnp.dot(rows_x, w_gate, preferred_element_type=jnp.float32)
        up = jnp.dot(rows_x, w_up, preferred_element_type=jnp.float32)
        sig = jax.nn.sigmoid(gate)
        act = gate * sig
        hidden = (coef_rows * act * up).astype(jnp.bfloat16)
        out_rows = jnp.dot(hidden, w_down, preferred_element_type=jnp.float32)
        out_sent = out_rows[half:].astype(jnp.bfloat16)
        rows_dy, out_sent = lax.optimization_barrier((rows_dy, out_sent))
        out_total = pair_sum(out_rows[:half], out_sent)

        dhid = jnp.dot(rows_dy, w_down.T, preferred_element_type=jnp.float32)
        scaled = coef_rows * dhid
        dgate = (scaled * up * sig * (1.0 + gate * (1.0 - sig))).astype(jnp.bfloat16)
        dup = (scaled * act).astype(jnp.bfloat16)
        dgate, blocks = tie(dgate, wave(out_total, {}, 1, "l"))
        out_carry = send(blocks)
        dx_rows = jnp.dot(dgate, w_gate.T, preferred_element_type=jnp.float32) + jnp.dot(
            dup, w_up.T, preferred_element_type=jnp.float32
        )
        dx_sent = dx_rows[half:].astype(jnp.bfloat16)
        hidden, dx_sent = lax.optimization_barrier((hidden, dx_sent))
        grad_down, mark = weight_grad(hidden, rows_dy, d, [])
        mark, out_carry = tie(mark, out_carry)
        dx_total = pair_sum(dx_rows[:half], dx_sent)
        dx_carry = {}

        grads, marks = [], [mark]
        work = [dgate, dup]
        for at in range(2, steps + 2):
            if at <= steps:
                out_carry.update(send(wave(out_total, out_carry, at, "l")))
            dx_blocks = wave(dx_total, dx_carry, at - 1, "r")
            if work:
                side, dx_blocks = tie(work.pop(0), dx_blocks)
                grad, mark = weight_grad(side, rows_wide, d, marks)
                grads.append(grad)
                if work and at <= steps:
                    mark, out_carry = tie(mark, out_carry)
                elif at <= steps:
                    zero = mark[0, 0].astype(jnp.bfloat16)
                    out_carry = {w: c + zero for w, c in out_carry.items()}
                marks = [mark]
            dx_carry.update(send(dx_blocks))
        for side in work:
            grads.append(weight_grad(side, rows_wide, d, marks)[0])
        grad_gate, grad_up = grads
        mixed, grad_tokens = (
            jnp.dot(select.T, final(total[0], carry), preferred_element_type=jnp.float32).astype(
                jnp.bfloat16
            )
            for total, carry in ((out_total, out_carry), (dx_total, dx_carry))
        )
        return (mixed, grad_tokens, grad_gate.T, grad_up.T, grad_down)

    return per_device


def solution(mesh):
    placed = (
        P(("groups", "et"), None),
        P(("groups", "et"), None),
        P(("groups", "et"), None),
        P(("groups", "et"), None),
        P(None, "et"),
        P(None, "et"),
        P("et", None),
    )
    return jax.shard_map(
        make_per_device(mesh.shape["et"]),
        mesh=mesh,
        in_specs=placed,
        out_specs=(
            P(("groups", "et"), None),
            P(("groups", "et"), None),
            P("groups", "et"),
            P("groups", "et"),
            P(("groups", "et"), None),
        ),
        check_vma=False,
    )
```
